32 devices in a mesh: slab: 8 (over z, core), deal: 4 (over y, x).
Axes of the slice: x: 2, y: 2, z: 4, core: 2. Of those that a mesh axis runs over, the one named last changes fastest.
Arguments:
- offsets: float32 [32768, 3, 128], P(('slab', 'deal')), may hold values from -0.5 to 0.5
- velocity: float32 [32768, 3, 128], P(('slab', 'deal')), may hold values from -6 to 6
- affine: float32 [32768, 9, 128], P(('slab', 'deal')), may hold values from -6 to 6
- particle_mass: float32 [32768, 128], P(('slab', 'deal')), may hold values from 0.5 to 2
- cell_in_tile: int32 [32768, 128], P(('slab', 'deal')), may hold values from 0 to 255
- block_tile: int32 [32768], P(('slab', 'deal')), may hold values from 0 to 2047, as said below
- live_blocks: int32 [8, 4], P('slab', 'deal'), may hold values from 512 to 1024, as said below
- send_lists: int32 [8, 4, 2, 16], P('slab', 'deal'), may hold values from 0 to 1023, as said below
- send_counts: int32 [8, 4, 2], P('slab', 'deal'), may hold values from 0 to 16, as said below
Outputs:
- updated_particles: float32 [32768, 15, 128], P(('slab', 'deal'))
- arrivals: float32 [8, 4, 2, 16, 16, 128], P('slab', 'deal')
- grid_velocity: float32 [3, 512, 8192], P(None, 'slab', 'deal')
The draws below stay inside these ranges and needn't reach their ends.
Inputs may be any that keep to these rules, and one draw needn't show every extreme that they name: `block_tile`: blocks are sorted by cell: on device (s, d) the tiles never fall along its blocks and lie in [max(d * R - M, 0), min((d + 1) * R + M, 2048)) with R = 512 and M = max(R // 16, 1); some device with d > 0 reaches d * R - M. `live_blocks`: some device has all 1024 blocks live. `send_lists`: the 32 entries of one device's two lists are distinct blocks of that device. `send_counts`: counts toward a slab beyond the ends are zero; some device sends 16 blocks downslope.
All inputs are finite; a program needn't handle non-finite values.
Results may differ from the reference program's by a relative error of at most 0.000073.
Values sent between devices are 32-bit elements; how exact they have to be, the bound alone decides.
A program may use at most 128 MiB of HBM per device.

```python
import math
import jax
import jax.numpy as jnp

NB = 1024
PX = 64
PLANE = 8192
TILE = 256
MIG = 16
SLABS = 8
DEALS = 4
BLOCKS = 32768
N_SLAB = 8
N_DEAL = 4


def draw_block_tile(key, part):
    tile_count = PX * PLANE // TILE
    share = tile_count // DEALS
    margin = max(share // 16, 1)
    key_raw, key_slab, key_deal = jax.random.split(jax.random.fold_in(key, 11), 3)
    deal_ids = jnp.arange(DEALS, dtype=jnp.int32)[None, :, None]
    lowest = jnp.maximum(deal_ids * share - margin, 0)
    highest = jnp.minimum((deal_ids + 1) * share + margin, tile_count)
    raw = jax.random.randint(key_raw, (SLABS, DEALS, NB), 0, 1 << 20)
    tiles = lowest + raw % (highest - lowest)
    tiles = jnp.sort(tiles, axis=-1)
    pick_slab = jax.random.randint(key_slab, (), 0, SLABS)
    pick_deal = jax.random.randint(key_deal, (), 1, DEALS)
    forced = (jnp.arange(SLABS)[:, None, None] == pick_slab) & (deal_ids == pick_deal) & (jnp.arange(NB)[None, None, :] == 0)
    tiles = jnp.where(forced, lowest, tiles)
    return tiles.reshape(BLOCKS).astype(jnp.int32)


def draw_live_blocks(key, part):
    key_counts, key_slab, key_deal = jax.random.split(key, 3)
    counts = jax.random.randint(key_counts, (SLABS, DEALS), NB // 2, NB + 1)
    pick_slab = jax.random.randint(key_slab, (), 0, SLABS)
    pick_deal = jax.random.randint(key_deal, (), 0, DEALS)
    chosen_cell = (jnp.arange(SLABS)[:, None] == pick_slab) & (jnp.arange(DEALS)[None, :] == pick_deal)
    return jnp.where(chosen_cell, NB, counts).astype(jnp.int32)


def draw_send_lists(key, part):
    scores = jax.random.randint(key, (SLABS, DEALS, NB), 0, 1 << 16)
    distinct = scores * NB + jnp.arange(NB, dtype=jnp.int32)
    ordering = jnp.argsort(distinct, axis=-1)
    return ordering[:, :, :2 * MIG].reshape(SLABS, DEALS, 2, MIG).astype(jnp.int32)


def draw_send_counts(key, part):
    key_counts, key_slab, key_deal = jax.random.split(key, 3)
    counts = jax.random.randint(key_counts, (SLABS, DEALS, 2), 0, MIG + 1)
    slab_ids = jnp.arange(SLABS)[:, None, None]
    deal_ids = jnp.arange(DEALS)[None, :, None]
    directions = jnp.arange(2)[None, None, :]
    counts = jnp.where((directions == 0) & (slab_ids == SLABS - 1), 0, counts)
    counts = jnp.where((directions == 1) & (slab_ids == 0), 0, counts)
    pick_slab = jax.random.randint(key_slab, (), 0, SLABS - 1)
    pick_deal = jax.random.randint(key_deal, (), 0, DEALS)
    forced = (slab_ids == pick_slab) & (deal_ids == pick_deal) & (directions == 0)
    return jnp.where(forced, MIG, counts).astype(jnp.int32)


def with_ends(drawn, key, least, top_value):
    longest = drawn.shape.index(max(drawn.shape))
    spots = []
    for shift in (0, 1):
        where = [jax.random.randint(jax.random.fold_in(key, axis), (), 0, length) for axis, length in enumerate(drawn.shape)]
        where[longest] = (where[longest] + shift) % drawn.shape[longest]
        spots.append(tuple(where))
    return drawn.at[spots[0]].set(least).at[spots[1]].set(top_value)


def level_of(key, shape, shards, low, largest):
    def one(position, blocks):
        steps = jax.random.uniform(jax.random.fold_in(jax.random.fold_in(key, 6), position), (blocks,), jnp.float32, low / len(shards), largest / len(shards))
        return jnp.repeat(jnp.exp(steps), shape[position] // blocks).reshape((-1,) + (1,) * (len(shape) - position - 1))

    loudness = one(*shards[0])
    for cut in shards[1:]:
        loudness = loudness * one(*cut)
    return loudness


def noise(key, shape, spread, most, cuts=(), kind=jnp.bfloat16):
    gain = level_of(key, shape, cuts, -0.22, 0.18) if cuts else 1.0
    entries = jax.random.normal(key, shape, jnp.float32) * spread * gain
    return jnp.minimum(jnp.maximum(entries, -most), most).astype(kind)


def setup_inputs(seed: int = 0) -> dict:
    splits = jax.random.split(jax.random.key(seed), 10)
    return {
        "offsets": jnp.clip(jax.random.uniform(splits[0], (BLOCKS, 3, 128), jnp.float32, -0.5, 0.5) * level_of(splits[0], (BLOCKS, 3, 128), ((0, 32),), -0.4, 0.0), -0.5, 0.5),
        "velocity": noise(splits[1], (BLOCKS, 3, 128), 1.0, 6.0, ((0, 32),), jnp.float32),
        "affine": noise(splits[2], (BLOCKS, 9, 128), 1.0, 6.0, ((0, 32),), jnp.float32),
        "particle_mass": jnp.clip(jnp.exp(math.log(2.0) - 1.3862944 * jax.random.uniform(splits[3], (BLOCKS, 128), jnp.float32) ** level_of(splits[3], (BLOCKS, 128), ((0, 32),), -0.2, 0.2)), 0.5, 2.0),
        "cell_in_tile": with_ends(jax.random.randint(splits[4], (BLOCKS, 128), 0, TILE), jax.random.fold_in(splits[4], 1), 0, TILE - 1).astype(jnp.int32),
        "block_tile": draw_block_tile(jax.random.fold_in(splits[9], 71), 0),
        "live_blocks": draw_live_blocks(jax.random.fold_in(splits[9], 71), 0),
        "send_lists": draw_send_lists(jax.random.fold_in(splits[9], 71), 0),
        "send_counts": draw_send_counts(jax.random.fold_in(splits[9], 71), 0),
    }


time_step = 0.1
viscosity = 0.2
gravity_pull = (3.0, 0.0, -5.0)


def momentum(offsets, velocity, affine):
    columns = []
    for column in range(3):
        total = velocity[:, column]
        for inner in range(3):
            total = total - affine[:, 3 * column + inner] * offsets[:, inner]
        columns.append(total)
    return jnp.stack(columns, axis=1)


def grid_update(summed):
    floor_mass = jnp.maximum(summed[0], 1.0)
    speeds = []
    for column in range(3):
        speeds.append(summed[1 + column] / floor_mass + time_step * gravity_pull[column])
    return jnp.stack(speeds, axis=0)


def smooth_planes(speed, padded):
    return speed + viscosity * (padded[:, 2:] + padded[:, :-2] - 2.0 * speed)


def new_state(offsets, moved):
    shifted = offsets + time_step * moved
    affine_rows = []
    for column in range(3):
        for inner in range(3):
            affine_rows.append(-4.0 * moved[:, column] * offsets[:, inner])
    return jnp.concatenate([shifted, moved, jnp.stack(affine_rows, axis=1)], axis=1)


def reference(offsets, velocity, affine, particle_mass, cell_in_tile, block_tile, live_blocks, send_lists, send_counts):
    cells_slab = PX * PLANE
    block_ids = jnp.arange(BLOCKS, dtype=jnp.int32)
    slab_of = block_ids // (NB * N_DEAL)
    live_flat = live_blocks.reshape(-1)
    active = ((block_ids % NB) < live_flat[block_ids // NB]).astype(jnp.float32)
    flat_cell = slab_of[:, None] * cells_slab + block_tile[:, None] * TILE + cell_in_tile
    weight = particle_mass * active[:, None]
    moment = momentum(offsets, velocity, affine)
    deposit = jnp.concatenate([weight[:, None, :], weight[:, None, :] * moment], axis=1)
    summed = jax.ops.segment_sum(jnp.transpose(deposit, (0, 2, 1)).reshape(-1, 4), flat_cell.reshape(-1), num_segments=N_SLAB * cells_slab)
    summed = summed.T.reshape(4, N_SLAB * PX, PLANE)
    speed = grid_update(summed)
    padded = jnp.pad(speed, ((0, 0), (1, 1), (0, 0)))
    settled = smooth_planes(speed, padded)
    picked = settled.reshape(3, -1)[:, flat_cell]
    moved = jnp.transpose(picked, (1, 0, 2))
    state = new_state(offsets, moved)
    records = jnp.concatenate([state, particle_mass[:, None, :]], axis=1)
    device_ids = jnp.arange(N_SLAB * N_DEAL, dtype=jnp.int32).reshape(N_SLAB, N_DEAL)
    gather_ids = device_ids[:, :, None, None] * NB + send_lists
    leaving = records[gather_ids]
    slots = jnp.arange(MIG, dtype=jnp.int32)
    keeping = (slots[None, None, None, :] < send_counts[..., None]).astype(jnp.float32)
    leaving = leaving * keeping[..., None, None]
    empty = jnp.zeros_like(leaving[:1, :, 0])
    from_left = jnp.concatenate([empty, leaving[:-1, :, 0]], axis=0)
    from_right = jnp.concatenate([leaving[1:, :, 1], empty], axis=0)
    arrivals = jnp.stack([from_left, from_right], axis=2)
    return state, arrivals, settled
```

```python
import functools

import jax
import jax.numpy as jnp
from jax import lax
from jax.experimental import pallas as pl
from jax.experimental.pallas import tpu as pltpu
from jax.sharding import PartitionSpec as P

PX = 64
PLANE = 8192
TILE = 256
LANES = 128

time_step = 0.1
viscosity = 0.2
gravity_pull = (3.0, 0.0, -5.0)

VMEM_LIMIT = 40 * 1024 * 1024


def deposit_kernel(tiles_ref, live_ref, off_ref, vel_ref, aff_ref, mass_ref, cell_ref,
                   acc_ref, down_ref, up_ref, *, blocks, unroll):
    step = pl.program_id(0)

    @pl.when(step == 0)
    def _():
        acc_ref[...] = jnp.zeros_like(acc_ref)

    slots = lax.broadcasted_iota(jnp.int32, (LANES, LANES), 0)
    half = lax.broadcasted_iota(jnp.int32, (8, LANES), 0) // 4
    live = live_ref[0]

    def group(i, carry):
        sums = []
        for u in range(unroll):
            b = i * unroll + u
            m = vel_ref[b]
            for j in range(3):
                m = m - aff_ref[b, pl.ds(j, 3, stride=3), :] * off_ref[b, j:j + 1, :]
            active = (step * blocks + b < live).astype(jnp.float32)
            w = mass_ref[pl.ds(b, 1), :] * active
            x = jnp.concatenate([w * m, w], axis=0)
            c = cell_ref[pl.ds(b, 1), :]
            x = jnp.where((c >> 7) == half, jnp.concatenate([x, x], axis=0), 0.0)
            high = x.astype(jnp.bfloat16).astype(jnp.float32)
            parts = jnp.concatenate([high, x - high], axis=0).astype(jnp.bfloat16)
            select = jnp.where((c & (LANES - 1)) == slots, 1.0, 0.0).astype(jnp.bfloat16)
            r = lax.dot_general(parts, select, (((1,), (1,)), ((), ())),
                                preferred_element_type=jnp.float32)
            sums.append(r[:8] + r[8:])
        for u in range(unroll):
            t = tiles_ref[step * blocks + i * unroll + u]
            acc_ref[t] += sums[u]
        return carry

    lax.fori_loop(0, blocks // unroll, group, 0)

    @pl.when(step == pl.num_programs(0) - 1)
    def _():
        n = down_ref.shape[0]
        down_ref[...] = acc_ref[acc_ref.shape[0] - n:]
        up_ref[...] = acc_ref[:n]


def picked_velocity(tile, c):
    where = jnp.broadcast_to(c & (LANES - 1), tile.shape)
    g = jnp.take_along_axis(tile, where, axis=1)
    return jnp.where(c >= LANES, g[4:7], g[0:3])


def write_state(out_ref, b, v, off_ref, src):
    o = off_ref[src]
    out_ref[b, 0:3, :] = o + time_step * v
    out_ref[b, 3:6, :] = v
    for j in range(3):
        out_ref[b, pl.ds(6 + j, 3, stride=3), :] = (-4.0 * v) * off_ref[src, j:j + 1, :]


def grid_kernel(tiles_ref, lists_ref, counts_ref, ends_ref, acc_ref, before_ref, after_ref,
                off_ref, mass_ref, cell_ref, settled_ref, cols_ref, rec_ref, speed_ref,
                *, row, margin):
    total = acc_ref.shape[0]
    side = before_ref.shape[0]
    rid = lax.broadcasted_iota(jnp.int32, (1, 8, LANES), 1)
    pull = jnp.zeros((1, 8, LANES), jnp.float32)
    for k in range(3):
        pull = jnp.where(rid % 4 == k, time_step * gravity_pull[k], pull)

    def speed_of(x):
        mass = jnp.where(rid < 4, x[:, 3:4, :], x[:, 7:8, :])
        return x / jnp.maximum(mass, 1.0) + pull

    first = ends_ref[0]
    last = ends_ref[1]
    inner = side - row
    chunk = 8

    def middle(i, carry):
        at = inner + i * chunk
        speed_ref[pl.ds(row + at, chunk)] = speed_of(acc_ref[pl.ds(at, chunk)])
        return carry

    lax.fori_loop(0, (total - 2 * inner) // chunk, middle, 0)

    keep_first = 1.0 - first.astype(jnp.float32)
    keep_last = 1.0 - last.astype(jnp.float32)

    def outer(i, carry):
        at = i * chunk
        speed_ref[pl.ds(at, chunk)] = speed_of(before_ref[pl.ds(at, chunk)]) * keep_first
        end = total + row + at
        speed_ref[pl.ds(end, chunk)] = (
            speed_of(after_ref[pl.ds(inner + at, chunk)]) * keep_last)
        return carry

    lax.fori_loop(0, row // chunk, outer, 0)

    def seam(i, carry):
        at = i * chunk
        beyond = at < margin * row
        x = speed_of(acc_ref[pl.ds(at, chunk)] + before_ref[pl.ds(row + at, chunk)])
        speed_ref[pl.ds(row + at, chunk)] = x * jnp.where(beyond, keep_first, 1.0)
        far = total - inner + at
        past = at >= inner - margin * row
        y = speed_of(acc_ref[pl.ds(far, chunk)] + after_ref[pl.ds(at, chunk)])
        speed_ref[pl.ds(row + far, chunk)] = y * jnp.where(past, keep_last, 1.0)
        return carry

    lax.fori_loop(0, inner // chunk, seam, 0)

    def smooth(i, carry):
        at = i * chunk
        s = speed_ref[pl.ds(row + at, chunk)]
        settled_ref[pl.ds(at, chunk)] = s + viscosity * (
            speed_ref[pl.ds(2 * row + at, chunk)] + speed_ref[pl.ds(at, chunk)] - 2.0 * s)
        return carry

    lax.fori_loop(0, total // chunk, smooth, 0)

    planes = cols_ref.shape[1]
    flat = settled_ref.reshape(total * 8, LANES)

    def column(tc, carry):
        for group in range(planes // 8):
            for h in range(2):
                for k in range(3):
                    start = (margin + group * 8) * row * 8 + tc * 8 + h * 4 + k
                    x = flat[pl.ds(start, 8, stride=row * 8), :]
                    at = pl.multiple_of(tc * TILE + h * LANES, LANES)
                    cols_ref[k, group * 8:group * 8 + 8, pl.ds(at, LANES)] = x
        return carry

    lax.fori_loop(0, row, column, 0)

    slots = lists_ref.shape[1]

    def record(i, carry):
        for way in range(2):
            b = lists_ref[way, i]
            keep = jnp.where(i < counts_ref[way], 1.0, 0.0)
            v = picked_velocity(settled_ref[tiles_ref[b]], cell_ref[pl.ds(b, 1), :])
            o = off_ref[b]
            at = way * slots + i
            rec_ref[at, 0:3, :] = (o + time_step * v) * keep
            rec_ref[at, 3:6, :] = v * keep
            for j in range(3):
                rec_ref[at, pl.ds(6 + j, 3, stride=3), :] = (
                    (-4.0 * v) * off_ref[b, j:j + 1, :] * keep)
            rec_ref[at, 15:16, :] = mass_ref[pl.ds(b, 1), :] * keep
        return carry

    lax.fori_loop(0, slots, record, 0)


def update_kernel(tiles_ref, off_ref, cell_ref, settled_ref, out_ref, *, blocks, unroll):
    step = pl.program_id(0)

    def group(i, carry):
        for u in range(unroll):
            b = i * unroll + u
            t = tiles_ref[step * blocks + b]
            v = picked_velocity(settled_ref[t], cell_ref[pl.ds(b, 1), :])
            write_state(out_ref, b, v, off_ref, b)
        return carry

    lax.fori_loop(0, blocks // unroll, group, 0)


def body(offsets, velocity, affine, particle_mass, cell_in_tile, block_tile, live_blocks,
         send_lists, send_counts):
    axes = ("slab", "deal")
    slabs, deals = lax.axis_size("slab"), lax.axis_size("deal")
    count = slabs * deals
    slab, deal = lax.axis_index("slab"), lax.axis_index("deal")
    nb = offsets.shape[0]
    row = PLANE // TILE
    planes = PX // deals
    share = planes * row
    margin = -(-max(share // 16, 1) // row)
    total = (planes + 2 * margin) * row
    side = (2 * margin + 1) * row
    f32 = jnp.float32

    tiles = block_tile - (deal * share - margin * row)
    blocks = 128 if nb % 128 == 0 else nb
    unroll = 8
    params = pltpu.CompilerParams(vmem_limit_bytes=VMEM_LIMIT)
    smem = pl.BlockSpec(memory_space=pltpu.SMEM)
    vmem = pl.BlockSpec(memory_space=pltpu.VMEM)

    def per_block(*tail):
        return pl.BlockSpec((blocks,) + tail, lambda i: (i,) + (0,) * len(tail))

    def whole(*shape):
        return pl.BlockSpec(shape, lambda i: (0,) * len(shape))

    acc, down, up = pl.pallas_call(
        functools.partial(deposit_kernel, blocks=blocks, unroll=unroll),
        grid=(nb // blocks,),
        in_specs=[smem, smem, per_block(3, LANES), per_block(3, LANES), per_block(9, LANES),
                  per_block(LANES), per_block(LANES)],
        out_specs=[whole(total, 8, LANES), whole(side, 8, LANES), whole(side, 8, LANES)],
        out_shape=[jax.ShapeDtypeStruct((n, 8, LANES), f32) for n in (total, side, side)],
        compiler_params=params,
        name="deposit",
    )(tiles, live_blocks.reshape(1), offsets, velocity, affine, particle_mass, cell_in_tile)

    before = lax.ppermute(down, axes, [(i, i + 1) for i in range(count - 1)])
    after = lax.ppermute(up, axes, [(i + 1, i) for i in range(count - 1)])

    place = slab * deals + deal
    ends = jnp.stack([place == 0, place == count - 1]).astype(jnp.int32)
    mig = send_lists.shape[-1]
    settled, cols, records = pl.pallas_call(
        functools.partial(grid_kernel, row=row, margin=margin),
        in_specs=[smem] * 4 + [vmem] * 6,
        out_specs=[vmem] * 3,
        out_shape=[jax.ShapeDtypeStruct((total, 8, LANES), f32),
                   jax.ShapeDtypeStruct((3, planes, PLANE), f32),
                   jax.ShapeDtypeStruct((2 * mig, 16, LANES), f32)],
        scratch_shapes=[pltpu.VMEM((total + 2 * row, 8, LANES), f32)],
        compiler_params=params,
        name="grid_step",
    )(tiles, send_lists[0, 0], send_counts.reshape(2), ends, acc, before, after,
      offsets, particle_mass, cell_in_tile)

    from_left = lax.ppermute(records[:mig], "slab", [(i, i + 1) for i in range(slabs - 1)])
    from_right = lax.ppermute(records[mig:], "slab", [(i + 1, i) for i in range(slabs - 1)])

    width = PLANE // deals
    pieces = [lax.dynamic_slice_in_dim(cols, deal * width, width, axis=2)]
    for k in range(1, deals):
        chosen = lax.dynamic_slice_in_dim(cols, ((deal + k) % deals) * width, width, axis=2)
        pieces.append(lax.ppermute(chosen, "deal", [(i, (i + k) % deals) for i in range(deals)]))

    state = pl.pallas_call(
        functools.partial(update_kernel, blocks=blocks, unroll=unroll),
        grid=(nb // blocks,),
        in_specs=[smem, per_block(3, LANES), per_block(LANES), whole(total, 8, LANES)],
        out_specs=per_block(15, LANES),
        out_shape=jax.ShapeDtypeStruct((nb, 15, LANES), f32),
        compiler_params=params,
        cost_estimate=pl.CostEstimate(flops=nb * 15 * LANES * 4,
                                      bytes_accessed=nb * 20 * LANES * 4, transcendentals=0),
        name="update",
    )(tiles, offsets, cell_in_tile, settled)

    arrivals = jnp.stack([from_left, from_right], axis=0)[None, None]
    grid = jnp.zeros((3, PX, width), f32)
    for k in range(deals):
        grid = lax.dynamic_update_slice_in_dim(
            grid, pieces[k], ((deal - k) % deals) * planes, axis=1)
    return state, arrivals, grid


def solution(mesh):
    placed = (
        P(("slab", "deal"), None, None),
        P(("slab", "deal"), None, None),
        P(("slab", "deal"), None, None),
        P(("slab", "deal"), None),
        P(("slab", "deal"), None),
        P(("slab", "deal")),
        P("slab", "deal"),
        P("slab", "deal", None, None),
        P("slab", "deal", None),
    )
    return jax.shard_map(
        body,
        mesh=mesh,
        in_specs=placed,
        out_specs=(
            P(("slab", "deal"), None, None),
            P("slab", "deal", None, None, None, None),
            P(None, "slab", "deal"),
        ),
        check_vma=False,
    )
```

```python
import functools

import jax
import jax.numpy as jnp
from jax import lax
from jax.experimental import pallas as pl
from jax.experimental.pallas import tpu as pltpu
from jax.sharding import PartitionSpec as P

PX = 64
PLANE = 8192
TILE = 256
LANES = 128
SPAN = 32

time_step = 0.1
viscosity = 0.2
gravity_pull = (3.0, 0.0, -5.0)

VMEM_LIMIT = 40 * 1024 * 1024


def deposit_span(at, first, start, stop, ins, out_ref, shift, tiles_ref, parts_ref):
    off_ref, vel_ref, aff_ref, mass_ref, cell_ref = ins
    slots = lax.broadcasted_iota(jnp.int32, (LANES, LANES), 0).astype(jnp.float32)
    slots = slots.astype(jnp.bfloat16)
    one, zero = jnp.ones((), jnp.bfloat16), jnp.zeros((), jnp.bfloat16)
    spot = lax.broadcasted_iota(jnp.int32, (8, LANES), 0)
    sums = []
    for g in range(SPAN // 8):
        rows = pl.ds(pl.multiple_of(at + g * 8, 8), 8)
        offset = [off_ref[k, rows, :] for k in range(3)]
        block = first + at + g * 8 + spot
        w = jnp.where((block >= start) & (block < stop), mass_ref[rows, :], 0.0)
        values = []
        for k in range(3):
            m = vel_ref[k, rows, :]
            for j in range(3):
                m = m - aff_ref[3 * k + j, rows, :] * offset[j]
            values.append(w * m)
        values.append(w)
        c = cell_ref[rows, :]
        upper = c >= LANES
        base = g * LANES
        for k in range(4):
            high = values[k].astype(jnp.bfloat16).astype(jnp.float32)
            low = values[k] - high
            for s, part in enumerate((high, low)):
                put = base + s * 64 + k * 8
                parts_ref[put:put + 8, :] = jnp.where(upper, 0.0, part)
                parts_ref[put + 32:put + 40, :] = jnp.where(upper, part, 0.0)
        lane = (c & (LANES - 1)).astype(jnp.float32)
        for u in range(8):
            lhs = parts_ref[pl.ds(base + u, 16, stride=8), :].astype(jnp.bfloat16)
            row = jnp.broadcast_to(lane[u:u + 1], (16, LANES)).astype(jnp.bfloat16)
            select = jnp.where(jnp.concatenate([row] * 8, axis=0) == slots, one, zero)
            r = lax.dot_general(lhs, select, (((1,), (1,)), ((), ())),
                                preferred_element_type=jnp.float32)
            sums.append(r[:8] + r[8:])
    for u in range(SPAN):
        block = first + at + u
        t = tiles_ref[block] - shift
        inside = (block >= start) & (block < stop)
        out_ref[jnp.where(inside, t, 0)] += sums[u]


def deposit_range(blocks, start, stop, ins, out_ref, shift, tiles_ref, parts_ref):
    first = pl.program_id(0) * blocks
    low = lax.div(jnp.clip(start - first, 0, blocks), SPAN)
    high = lax.div(jnp.clip(stop - first, 0, blocks) + SPAN - 1, SPAN)
    high = jnp.where(stop > start, high, low)

    def step(i, carry):
        deposit_span(i * SPAN, first, start, stop, ins, out_ref, shift, tiles_ref, parts_ref)
        return carry

    lax.fori_loop(low, high, step, 0)


def edge_kernel(marks_ref, tiles_ref, *refs, blocks, shift):
    *ins, up_ref, down_ref, parts_ref = refs

    @pl.when(pl.program_id(0) == 0)
    def _():
        up_ref[...] = jnp.zeros_like(up_ref)
        down_ref[...] = jnp.zeros_like(down_ref)

    deposit_range(blocks, 0, marks_ref[0], ins, up_ref, 0, tiles_ref, parts_ref)
    deposit_range(blocks, marks_ref[1], marks_ref[2], ins, down_ref, shift, tiles_ref, parts_ref)


def middle_kernel(marks_ref, tiles_ref, *refs, blocks, shift):
    *ins, mid_ref, parts_ref = refs

    @pl.when(pl.program_id(0) == 0)
    def _():
        mid_ref[...] = jnp.zeros_like(mid_ref)

    deposit_range(blocks, marks_ref[0], marks_ref[1], ins, mid_ref, shift, tiles_ref, parts_ref)


def update_kernel(tiles_ref, off_ref, cell_ref, settled_ref, out_ref, picked_ref, *, blocks):
    first = pl.program_id(0) * blocks

    def step(i, carry):
        for g in range(SPAN // 8):
            rows = pl.ds(pl.multiple_of(i * SPAN + g * 8, 8), 8)
            c = cell_ref[rows, :]
            lane = c & (LANES - 1)
            base = g * 64
            for u in range(8):
                tile = settled_ref[tiles_ref[first + i * SPAN + g * 8 + u]]
                where = jnp.broadcast_to(lane[u:u + 1], (8, LANES))
                put = base + u * 8
                picked_ref[put:put + 8, :] = jnp.take_along_axis(tile, where, axis=1)
            offset = [off_ref[k, rows, :] for k in range(3)]
            for k in range(3):
                v = jnp.where(c >= LANES, picked_ref[pl.ds(base + 4 + k, 8, stride=8), :],
                              picked_ref[pl.ds(base + k, 8, stride=8), :])
                out_ref[k, rows, :] = offset[k] + time_step * v
                out_ref[3 + k, rows, :] = v
                for j in range(3):
                    out_ref[6 + 3 * k + j, rows, :] = (-4.0 * v) * offset[j]
        return carry

    lax.fori_loop(0, blocks // SPAN, step, 0)


def grid_kernel(tiles_ref, lists_ref, counts_ref, ends_ref, up_ref, mid_ref, down_ref,
                before_ref, after_ref, off_ref, mass_ref, cell_ref,
                settled_ref, cols_ref, rec_ref, speed_ref, *, row, margin):
    total = settled_ref.shape[0]
    side = before_ref.shape[0]
    inner = side - row
    rid = lax.broadcasted_iota(jnp.int32, (1, 8, LANES), 1)
    pull = jnp.zeros((1, 8, LANES), jnp.float32)
    for k in range(3):
        pull = jnp.where(rid % 4 == k, time_step * gravity_pull[k], pull)

    def speed_of(x):
        mass = jnp.where(rid < 4, x[:, 3:4, :], x[:, 7:8, :])
        return x / jnp.maximum(mass, 1.0) + pull

    chunk = 8
    keep_first = 1.0 - ends_ref[0].astype(jnp.float32)
    keep_last = 1.0 - ends_ref[1].astype(jnp.float32)
    far = row + total - side

    def middle(i, carry):
        at = i * chunk
        speed_ref[pl.ds(row + side + at, chunk)] = speed_of(mid_ref[pl.ds(at, chunk)])
        return carry

    lax.fori_loop(0, mid_ref.shape[0] // chunk, middle, 0)

    def outer(i, carry):
        at = i * chunk
        speed_ref[pl.ds(at, chunk)] = speed_of(before_ref[pl.ds(at, chunk)]) * keep_first
        speed_ref[pl.ds(side + at, chunk)] = speed_of(up_ref[pl.ds(inner + at, chunk)])
        speed_ref[pl.ds(far + at, chunk)] = speed_of(down_ref[pl.ds(at, chunk)])
        speed_ref[pl.ds(row + total + at, chunk)] = (
            speed_of(after_ref[pl.ds(inner + at, chunk)]) * keep_last)
        return carry

    lax.fori_loop(0, row // chunk, outer, 0)

    def seam(i, carry):
        at = i * chunk
        x = speed_of(up_ref[pl.ds(at, chunk)] + before_ref[pl.ds(row + at, chunk)])
        speed_ref[pl.ds(row + at, chunk)] = x * jnp.where(at < margin * row, keep_first, 1.0)
        y = speed_of(down_ref[pl.ds(row + at, chunk)] + after_ref[pl.ds(at, chunk)])
        past = at >= inner - margin * row
        speed_ref[pl.ds(far + row + at, chunk)] = y * jnp.where(past, keep_last, 1.0)
        return carry

    lax.fori_loop(0, inner // chunk, seam, 0)

    def smooth(i, carry):
        at = i * chunk
        s = speed_ref[pl.ds(row + at, chunk)]
        settled_ref[pl.ds(at, chunk)] = s + viscosity * (
            speed_ref[pl.ds(2 * row + at, chunk)] + speed_ref[pl.ds(at, chunk)] - 2.0 * s)
        return carry

    lax.fori_loop(0, total // chunk, smooth, 0)

    planes = cols_ref.shape[1]
    flat = settled_ref.reshape(total * 8, LANES)

    def column(tc, carry):
        for group in range(planes // 8):
            for h in range(2):
                for k in range(3):
                    start = (margin + group * 8) * row * 8 + tc * 8 + h * 4 + k
                    x = flat[pl.ds(start, 8, stride=row * 8), :]
                    at = pl.multiple_of(tc * TILE + h * LANES, LANES)
                    cols_ref[k, group * 8:group * 8 + 8, pl.ds(at, LANES)] = x
        return carry

    lax.fori_loop(0, row, column, 0)

    slots = lists_ref.shape[1]

    def record(i, carry):
        for way in range(2):
            b = lists_ref[way, i]
            keep = jnp.where(i < counts_ref[way], 1.0, 0.0)
            c = cell_ref[pl.ds(b, 1), :]
            tile = settled_ref[tiles_ref[b]]
            lane = jnp.broadcast_to(c & (LANES - 1), (8, LANES))
            g = jnp.take_along_axis(tile, lane, axis=1)
            v = jnp.where(c >= LANES, g[4:7], g[0:3])
            at = way * slots + i
            for k in range(3):
                o = off_ref[k, pl.ds(b, 1), :]
                rec_ref[at, k:k + 1, :] = (o + time_step * v[k:k + 1]) * keep
                rec_ref[at, pl.ds(6 + k, 3, stride=3), :] = ((-4.0 * v) * o) * keep
            rec_ref[at, 3:6, :] = v * keep
            rec_ref[at, 15:16, :] = mass_ref[pl.ds(b, 1), :] * keep
        return carry

    lax.fori_loop(0, slots, record, 0)


def body(offsets, velocity, affine, particle_mass, cell_in_tile, block_tile, live_blocks,
         send_lists, send_counts):
    axes = ("slab", "deal")
    slabs, deals = lax.axis_size("slab"), lax.axis_size("deal")
    count = slabs * deals
    slab, deal = lax.axis_index("slab"), lax.axis_index("deal")
    nb = offsets.shape[0]
    row = PLANE // TILE
    planes = PX // deals
    share = planes * row
    margin = -(-max(share // 16, 1) // row)
    total = (planes + 2 * margin) * row
    side = (2 * margin + 1) * row
    f32 = jnp.float32

    tiles = block_tile - (deal * share - margin * row)
    live = live_blocks[0, 0]
    low = jnp.minimum(jnp.sum((tiles < side).astype(jnp.int32)), live)
    high = jnp.minimum(jnp.sum((tiles < total - side).astype(jnp.int32)), live)
    marks = jnp.stack([low, high, live])
    offsets, velocity, affine = (jnp.transpose(x, (1, 0, 2)) for x in (offsets, velocity, affine))
    blocks = 128 if nb % 128 == 0 else nb
    steps = nb // blocks
    params = pltpu.CompilerParams(vmem_limit_bytes=VMEM_LIMIT)
    smem = pl.BlockSpec(memory_space=pltpu.SMEM)
    vmem = pl.BlockSpec(memory_space=pltpu.VMEM)

    def edge_chunk(i, marks_ref):
        held = jnp.maximum(lax.div(marks_ref[0] + blocks - 1, blocks) - 1, 0)
        used = (i * blocks < marks_ref[0]) | ((i + 1) * blocks > marks_ref[1])
        return jnp.where(used, i, held)

    def middle_chunk(i, marks_ref):
        first = jnp.minimum(lax.div(marks_ref[0], blocks), steps - 1)
        last = jnp.maximum(lax.div(marks_ref[1] + blocks - 1, blocks) - 1, first)
        return jnp.clip(i, first, last)

    def deposit(kernel, chunk, sizes, shift, name):
        def part(*lead):
            return pl.BlockSpec(lead + (blocks, LANES),
                                lambda i, m, t: (0,) * len(lead) + (chunk(i, m), 0))

        return pl.pallas_call(
            functools.partial(kernel, blocks=blocks, shift=shift),
            grid_spec=pltpu.PrefetchScalarGridSpec(
                num_scalar_prefetch=2,
                grid=(steps,),
                in_specs=[part(3), part(3), part(9), part(), part()],
                out_specs=[pl.BlockSpec((n, 8, LANES), lambda i, m, t: (0, 0, 0)) for n in sizes],
                scratch_shapes=[pltpu.VMEM((SPAN * 16, LANES), f32)],
            ),
            out_shape=[jax.ShapeDtypeStruct((n, 8, LANES), f32) for n in sizes],
            compiler_params=params,
            cost_estimate=pl.CostEstimate(flops=nb * 16 * LANES * LANES, transcendentals=0,
                                          bytes_accessed=nb * 17 * LANES * 4),
            name=name,
        )(marks, tiles, offsets, velocity, affine, particle_mass, cell_in_tile)

    up, down = deposit(edge_kernel, edge_chunk, (side, side), total - side, "deposit_edges")
    before = lax.ppermute(down, axes, [(i, i + 1) for i in range(count - 1)])
    after = lax.ppermute(up, axes, [(i + 1, i) for i in range(count - 1)])
    mid, = deposit(middle_kernel, middle_chunk, (total - 2 * side,), side, "deposit_middle")

    place = slab * deals + deal
    ends = jnp.stack([place == 0, place == count - 1]).astype(jnp.int32)
    mig = send_lists.shape[-1]
    settled, cols, records = pl.pallas_call(
        functools.partial(grid_kernel, row=row, margin=margin),
        in_specs=[smem] * 4 + [vmem] * 8,
        out_specs=[vmem] * 3,
        out_shape=[jax.ShapeDtypeStruct((total, 8, LANES), f32),
                   jax.ShapeDtypeStruct((3, planes, PLANE), f32),
                   jax.ShapeDtypeStruct((2 * mig, 16, LANES), f32)],
        scratch_shapes=[pltpu.VMEM((total + 2 * row, 8, LANES), f32)],
        compiler_params=params,
        name="grid_step",
    )(tiles, send_lists[0, 0], send_counts.reshape(2), ends, up, mid, down, before, after,
      offsets, particle_mass, cell_in_tile)

    from_left = lax.ppermute(records[:mig], "slab", [(i, i + 1) for i in range(slabs - 1)])
    from_right = lax.ppermute(records[mig:], "slab", [(i + 1, i) for i in range(slabs - 1)])

    width = PLANE // deals
    pieces = [lax.dynamic_slice_in_dim(cols, deal * width, width, axis=2)]
    for k in range(1, deals):
        chosen = lax.dynamic_slice_in_dim(cols, ((deal + k) % deals) * width, width, axis=2)
        pieces.append(lax.ppermute(chosen, "deal", [(i, (i + k) % deals) for i in range(deals)]))

    state = pl.pallas_call(
        functools.partial(update_kernel, blocks=blocks),
        grid=(steps,),
        in_specs=[smem, pl.BlockSpec((3, blocks, LANES), lambda i: (0, i, 0)),
                  pl.BlockSpec((blocks, LANES), lambda i: (i, 0)),
                  pl.BlockSpec((total, 8, LANES), lambda i: (0, 0, 0))],
        out_specs=pl.BlockSpec((15, blocks, LANES), lambda i: (0, i, 0)),
        out_shape=jax.ShapeDtypeStruct((15, nb, LANES), f32),
        scratch_shapes=[pltpu.VMEM((SPAN * 8, LANES), f32)],
        compiler_params=params,
        cost_estimate=pl.CostEstimate(flops=nb * 15 * LANES * 4,
                                      bytes_accessed=nb * 20 * LANES * 4, transcendentals=0),
        name="update",
    )(tiles, offsets, cell_in_tile, settled)
    state = jnp.transpose(state, (1, 0, 2))

    arrivals = jnp.stack([from_left, from_right], axis=0)[None, None]
    grid = jnp.zeros((3, PX, width), f32)
    for k in range(deals):
        grid = lax.dynamic_update_slice_in_dim(
            grid, pieces[k], ((deal - k) % deals) * planes, axis=1)
    return state, arrivals, grid


def solution(mesh):
    placed = (
        P(("slab", "deal"), None, None),
        P(("slab", "deal"), None, None),
        P(("slab", "deal"), None, None),
        P(("slab", "deal"), None),
        P(("slab", "deal"), None),
        P(("slab", "deal")),
        P("slab", "deal"),
        P("slab", "deal", None, None),
        P("slab", "deal", None),
    )
    return jax.shard_map(
        body,
        mesh=mesh,
        in_specs=placed,
        out_specs=(
            P(("slab", "deal"), None, None),
            P("slab", "deal", None, None, None, None),
            P(None, "slab", "deal"),
        ),
        check_vma=False,
    )
```

```python
import functools

import jax
import jax.numpy as jnp
from jax import lax
from jax.experimental import pallas as pl
from jax.experimental.pallas import tpu as pltpu
from jax.sharding import PartitionSpec as P

PX = 64
PLANE = 8192
TILE = 256
LANES = 128
SPAN = 32

time_step = 0.1
viscosity = 0.2
gravity_pull = (3.0, 0.0, -5.0)

VMEM_LIMIT = 60 * 1024 * 1024


def deposit_span(at, first, start, stop, ins, out_ref, shift, tiles_ref, parts_ref):
    off_ref, vel_ref, aff_ref, mass_ref, cell_ref = ins
    slots = lax.broadcasted_iota(jnp.int32, (LANES, LANES), 0).astype(jnp.float32)
    slots = slots.astype(jnp.bfloat16)
    one, zero = jnp.ones((), jnp.bfloat16), jnp.zeros((), jnp.bfloat16)
    spot = lax.broadcasted_iota(jnp.int32, (8, LANES), 0)
    sums = []
    for g in range(SPAN // 8):
        rows = pl.ds(pl.multiple_of(at + g * 8, 8), 8)
        offset = [off_ref[k, rows, :] for k in range(3)]
        block = first + at + g * 8 + spot
        w = jnp.where((block >= start) & (block < stop), mass_ref[rows, :], 0.0)
        values = []
        for k in range(3):
            m = vel_ref[k, rows, :]
            for j in range(3):
                m = m - aff_ref[3 * k + j, rows, :] * offset[j]
            values.append(w * m)
        values.append(w)
        c = cell_ref[rows, :]
        upper = c >= LANES
        base = g * LANES
        for k in range(4):
            high = values[k].astype(jnp.bfloat16).astype(jnp.float32)
            low = values[k] - high
            for s, part in enumerate((high, low)):
                put = base + s * 64 + k * 8
                parts_ref[put:put + 8, :] = jnp.where(upper, 0.0, part)
                parts_ref[put + 32:put + 40, :] = jnp.where(upper, part, 0.0)
        lane = (c & (LANES - 1)).astype(jnp.float32)
        for u in range(8):
            lhs = parts_ref[pl.ds(base + u, 16, stride=8), :].astype(jnp.bfloat16)
            row = jnp.broadcast_to(lane[u:u + 1], (16, LANES)).astype(jnp.bfloat16)
            select = jnp.where(jnp.concatenate([row] * 8, axis=0) == slots, one, zero)
            r = lax.dot_general(lhs, select, (((1,), (1,)), ((), ())),
                                preferred_element_type=jnp.float32)
            sums.append(r[:8] + r[8:])
    for u in range(SPAN):
        block = first + at + u
        t = tiles_ref[block] - shift
        inside = (block >= start) & (block < stop)
        out_ref[jnp.where(inside, t, 0)] += sums[u]


def deposit_range(blocks, start, stop, ins, out_ref, shift, tiles_ref, parts_ref):
    first = pl.program_id(0) * blocks
    low = lax.div(jnp.clip(start - first, 0, blocks), SPAN)
    high = lax.div(jnp.clip(stop - first, 0, blocks) + SPAN - 1, SPAN)
    high = jnp.where(stop > start, high, low)

    def step(i, carry):
        deposit_span(i * SPAN, first, start, stop, ins, out_ref, shift, tiles_ref, parts_ref)
        return carry

    lax.fori_loop(low, high, step, 0)


def edge_kernel(marks_ref, tiles_ref, *refs, blocks, shift):
    *ins, up_ref, down_ref, parts_ref = refs

    @pl.when(pl.program_id(0) == 0)
    def _():
        up_ref[...] = jnp.zeros_like(up_ref)
        down_ref[...] = jnp.zeros_like(down_ref)

    deposit_range(blocks, 0, marks_ref[0], ins, up_ref, 0, tiles_ref, parts_ref)
    deposit_range(blocks, marks_ref[1], marks_ref[2], ins, down_ref, shift, tiles_ref, parts_ref)


def middle_kernel(marks_ref, tiles_ref, *refs, blocks, shift):
    *ins, mid_ref, parts_ref = refs

    @pl.when(pl.program_id(0) == 0)
    def _():
        mid_ref[...] = jnp.zeros_like(mid_ref)

    deposit_range(blocks, marks_ref[0], marks_ref[1], ins, mid_ref, shift, tiles_ref, parts_ref)


def update_kernel(tiles_ref, off_ref, cell_ref, settled_ref, out_ref, picked_ref, *, blocks):
    first = pl.program_id(0) * blocks

    def step(i, carry):
        for g in range(SPAN // 8):
            rows = pl.ds(pl.multiple_of(i * SPAN + g * 8, 8), 8)
            c = cell_ref[rows, :]
            lane = c & (LANES - 1)
            base = g * 64
            for u in range(8):
                tile = settled_ref[tiles_ref[first + i * SPAN + g * 8 + u]]
                where = jnp.broadcast_to(lane[u:u + 1], (8, LANES))
                put = base + u * 8
                picked_ref[put:put + 8, :] = jnp.take_along_axis(tile, where, axis=1)
            offset = [off_ref[k, rows, :] for k in range(3)]
            for k in range(3):
                v = jnp.where(c >= LANES, picked_ref[pl.ds(base + 4 + k, 8, stride=8), :],
                              picked_ref[pl.ds(base + k, 8, stride=8), :])
                out_ref[k, rows, :] = offset[k] + time_step * v
                out_ref[3 + k, rows, :] = v
                for j in range(3):
                    out_ref[6 + 3 * k + j, rows, :] = (-4.0 * v) * offset[j]
        return carry

    lax.fori_loop(0, blocks // SPAN, step, 0)


def grid_kernel(tiles_ref, lists_ref, counts_ref, ends_ref, up_ref, mid_ref, down_ref,
                before_ref, after_ref, off_ref, mass_ref, cell_ref,
                settled_ref, *refs, row, margin, deals):
    *piece_refs, rec_down_ref, rec_up_ref, speed_ref = refs
    rec_refs = (rec_down_ref, rec_up_ref)
    total = settled_ref.shape[0]
    side = before_ref.shape[0]
    inner = side - row
    rid = lax.broadcasted_iota(jnp.int32, (1, 8, LANES), 1)
    pull = jnp.zeros((1, 8, LANES), jnp.float32)
    for k in range(3):
        pull = jnp.where(rid % 4 == k, time_step * gravity_pull[k], pull)

    def speed_of(x):
        mass = jnp.where(rid < 4, x[:, 3:4, :], x[:, 7:8, :])
        return x / jnp.maximum(mass, 1.0) + pull

    chunk = 8
    keep_first = 1.0 - ends_ref[0].astype(jnp.float32)
    keep_last = 1.0 - ends_ref[1].astype(jnp.float32)
    far = row + total - side

    def middle(i, carry):
        at = i * chunk
        speed_ref[pl.ds(row + side + at, chunk)] = speed_of(mid_ref[pl.ds(at, chunk)])
        return carry

    lax.fori_loop(0, mid_ref.shape[0] // chunk, middle, 0)

    def outer(i, carry):
        at = i * chunk
        speed_ref[pl.ds(at, chunk)] = speed_of(before_ref[pl.ds(at, chunk)]) * keep_first
        speed_ref[pl.ds(side + at, chunk)] = speed_of(up_ref[pl.ds(inner + at, chunk)])
        speed_ref[pl.ds(far + at, chunk)] = speed_of(down_ref[pl.ds(at, chunk)])
        speed_ref[pl.ds(row + total + at, chunk)] = (
            speed_of(after_ref[pl.ds(inner + at, chunk)]) * keep_last)
        return carry

    lax.fori_loop(0, row // chunk, outer, 0)

    def seam(i, carry):
        at = i * chunk
        x = speed_of(up_ref[pl.ds(at, chunk)] + before_ref[pl.ds(row + at, chunk)])
        speed_ref[pl.ds(row + at, chunk)] = x * jnp.where(at < margin * row, keep_first, 1.0)
        y = speed_of(down_ref[pl.ds(row + at, chunk)] + after_ref[pl.ds(at, chunk)])
        past = at >= inner - margin * row
        speed_ref[pl.ds(far + row + at, chunk)] = y * jnp.where(past, keep_last, 1.0)
        return carry

    lax.fori_loop(0, inner // chunk, seam, 0)

    def smooth(i, carry):
        at = i * chunk
        s = speed_ref[pl.ds(row + at, chunk)]
        settled_ref[pl.ds(at, chunk)] = s + viscosity * (
            speed_ref[pl.ds(2 * row + at, chunk)] + speed_ref[pl.ds(at, chunk)] - 2.0 * s)
        return carry

    lax.fori_loop(0, total // chunk, smooth, 0)

    flat = settled_ref.reshape(total * 8, LANES)
    planes = piece_refs[0].shape[1]
    across = row // deals
    for turn in range(deals):
        piece_ref = piece_refs[turn]
        corner = lax.rem(ends_ref[2] + turn, deals) * across

        def column(tc, carry, piece_ref=piece_ref, corner=corner):
            for group in range(planes // 8):
                for h in range(2):
                    for k in range(3):
                        start = (margin + group * 8) * row * 8 + (corner + tc) * 8 + h * 4 + k
                        x = flat[pl.ds(start, 8, stride=row * 8), :]
                        at = pl.multiple_of(tc * TILE + h * LANES, LANES)
                        piece_ref[k, group * 8:group * 8 + 8, pl.ds(at, LANES)] = x
            return carry

        lax.fori_loop(0, across, column, 0)

    slots = lists_ref.shape[1]

    def record(i, carry):
        for way in range(2):
            b = lists_ref[way, i]
            keep = jnp.where(i < counts_ref[way], 1.0, 0.0)
            c = cell_ref[pl.ds(b, 1), :]
            tile = settled_ref[tiles_ref[b]]
            lane = jnp.broadcast_to(c & (LANES - 1), (8, LANES))
            g = jnp.take_along_axis(tile, lane, axis=1)
            v = jnp.where(c >= LANES, g[4:7], g[0:3])
            rec_ref = rec_refs[way]
            for k in range(3):
                o = off_ref[k, pl.ds(b, 1), :]
                rec_ref[i, k:k + 1, :] = (o + time_step * v[k:k + 1]) * keep
                rec_ref[i, pl.ds(6 + k, 3, stride=3), :] = ((-4.0 * v) * o) * keep
            rec_ref[i, 3:6, :] = v * keep
            rec_ref[i, 15:16, :] = mass_ref[pl.ds(b, 1), :] * keep
        return carry

    lax.fori_loop(0, slots, record, 0)


def assemble_kernel(deal_ref, *refs, deals):
    *piece_refs, left_ref, right_ref, grid_ref, arrivals_ref, sems = refs
    planes = piece_refs[0].shape[1]
    copies = []
    for turn, piece_ref in enumerate(piece_refs):
        slot = lax.rem(deal_ref[0] - turn + deals, deals)
        rows = pl.ds(pl.multiple_of(slot * planes, 8), planes)
        copies.append((piece_ref, grid_ref.at[:, rows, :]))
    copies.append((left_ref, arrivals_ref.at[0]))
    copies.append((right_ref, arrivals_ref.at[1]))
    started = [pltpu.make_async_copy(a, b, sems.at[i]) for i, (a, b) in enumerate(copies)]
    for c in started:
        c.start()
    for c in started:
        c.wait()


def body(offsets, velocity, affine, particle_mass, cell_in_tile, block_tile, live_blocks,
         send_lists, send_counts):
    axes = ("slab", "deal")
    slabs, deals = lax.axis_size("slab"), lax.axis_size("deal")
    count = slabs * deals
    slab, deal = lax.axis_index("slab"), lax.axis_index("deal")
    nb = offsets.shape[0]
    row = PLANE // TILE
    planes = PX // deals
    share = planes * row
    margin = -(-max(share // 16, 1) // row)
    total = (planes + 2 * margin) * row
    side = (2 * margin + 1) * row
    f32 = jnp.float32

    tiles = block_tile - (deal * share - margin * row)
    live = live_blocks[0, 0]
    low = jnp.minimum(jnp.sum((tiles < side).astype(jnp.int32)), live)
    high = jnp.minimum(jnp.sum((tiles < total - side).astype(jnp.int32)), live)
    marks = jnp.stack([low, high, live])
    offsets, velocity, affine = (jnp.transpose(x, (1, 0, 2)) for x in (offsets, velocity, affine))
    blocks = 128 if nb % 128 == 0 else nb
    steps = nb // blocks
    params = pltpu.CompilerParams(vmem_limit_bytes=VMEM_LIMIT)
    smem = pl.BlockSpec(memory_space=pltpu.SMEM)
    vmem = pl.BlockSpec(memory_space=pltpu.VMEM)

    def edge_chunk(i, marks_ref):
        held = jnp.maximum(lax.div(marks_ref[0] + blocks - 1, blocks) - 1, 0)
        used = (i * blocks < marks_ref[0]) | ((i + 1) * blocks > marks_ref[1])
        return jnp.where(used, i, held)

    def middle_chunk(i, marks_ref):
        first = jnp.minimum(lax.div(marks_ref[0], blocks), steps - 1)
        last = jnp.maximum(lax.div(marks_ref[1] + blocks - 1, blocks) - 1, first)
        return jnp.clip(i, first, last)

    def deposit(kernel, chunk, sizes, shift, name):
        def part(*lead):
            return pl.BlockSpec(lead + (blocks, LANES),
                                lambda i, m, t: (0,) * len(lead) + (chunk(i, m), 0))

        return pl.pallas_call(
            functools.partial(kernel, blocks=blocks, shift=shift),
            grid_spec=pltpu.PrefetchScalarGridSpec(
                num_scalar_prefetch=2,
                grid=(steps,),
                in_specs=[part(3), part(3), part(9), part(), part()],
                out_specs=[pl.BlockSpec((n, 8, LANES), lambda i, m, t: (0, 0, 0)) for n in sizes],
                scratch_shapes=[pltpu.VMEM((SPAN * 16, LANES), f32)],
            ),
            out_shape=[jax.ShapeDtypeStruct((n, 8, LANES), f32) for n in sizes],
            compiler_params=params,
            cost_estimate=pl.CostEstimate(flops=nb * 16 * LANES * LANES, transcendentals=0,
                                          bytes_accessed=nb * 17 * LANES * 4),
            name=name,
        )(marks, tiles, offsets, velocity, affine, particle_mass, cell_in_tile)

    up, down = deposit(edge_kernel, edge_chunk, (side, side), total - side, "deposit_edges")
    before = lax.ppermute(down, axes, [(i, i + 1) for i in range(count - 1)])
    after = lax.ppermute(up, axes, [(i + 1, i) for i in range(count - 1)])
    mid, = deposit(middle_kernel, middle_chunk, (total - 2 * side,), side, "deposit_middle")

    place = slab * deals + deal
    ends = jnp.stack([place == 0, place == count - 1, deal]).astype(jnp.int32)
    mig = send_lists.shape[-1]
    width = PLANE // deals
    outs = ([jax.ShapeDtypeStruct((total, 8, LANES), f32)]
            + [jax.ShapeDtypeStruct((3, planes, width), f32)] * deals
            + [jax.ShapeDtypeStruct((mig, 16, LANES), f32)] * 2)
    settled, *pieces, leave_down, leave_up = pl.pallas_call(
        functools.partial(grid_kernel, row=row, margin=margin, deals=deals),
        in_specs=[smem] * 4 + [vmem] * 8,
        out_specs=[vmem] * len(outs),
        out_shape=outs,
        scratch_shapes=[pltpu.VMEM((total + 2 * row, 8, LANES), f32)],
        compiler_params=params,
        name="grid_step",
    )(tiles, send_lists[0, 0], send_counts.reshape(2), ends, up, mid, down, before, after,
      offsets, particle_mass, cell_in_tile)

    for k in range(1, deals):
        pairs = [(i, (i + k) % deals) for i in range(deals)]
        pieces[k] = lax.ppermute(pieces[k], "deal", pairs)
    from_left = lax.ppermute(leave_down, "slab", [(i, i + 1) for i in range(slabs - 1)])
    from_right = lax.ppermute(leave_up, "slab", [(i + 1, i) for i in range(slabs - 1)])

    state = pl.pallas_call(
        functools.partial(update_kernel, blocks=blocks),
        grid=(steps,),
        in_specs=[smem, pl.BlockSpec((3, blocks, LANES), lambda i: (0, i, 0)),
                  pl.BlockSpec((blocks, LANES), lambda i: (i, 0)),
                  pl.BlockSpec((total, 8, LANES), lambda i: (0, 0, 0))],
        out_specs=pl.BlockSpec((15, blocks, LANES), lambda i: (0, i, 0)),
        out_shape=jax.ShapeDtypeStruct((15, nb, LANES), f32),
        scratch_shapes=[pltpu.VMEM((SPAN * 8, LANES), f32)],
        compiler_params=params,
        cost_estimate=pl.CostEstimate(flops=nb * 15 * LANES * 4,
                                      bytes_accessed=nb * 20 * LANES * 4, transcendentals=0),
        name="update",
    )(tiles, offsets, cell_in_tile, settled)
    state = jnp.transpose(state, (1, 0, 2))

    anywhere = pl.BlockSpec(memory_space=pl.ANY)
    grid, arrivals = pl.pallas_call(
        functools.partial(assemble_kernel, deals=deals),
        in_specs=[smem] + [anywhere] * (deals + 2),
        out_specs=[anywhere] * 2,
        out_shape=[jax.ShapeDtypeStruct((3, PX, width), f32),
                   jax.ShapeDtypeStruct((2, mig, 16, LANES), f32)],
        scratch_shapes=[pltpu.SemaphoreType.DMA((deals + 2,))],
        compiler_params=pltpu.CompilerParams(vmem_limit_bytes=VMEM_LIMIT // 4),
        name="assemble",
    )(ends[2:], *pieces, from_left, from_right)
    arrivals = arrivals[None, None]
    return state, arrivals, grid


def solution(mesh):
    placed = (
        P(("slab", "deal"), None, None),
        P(("slab", "deal"), None, None),
        P(("slab", "deal"), None, None),
        P(("slab", "deal"), None),
        P(("slab", "deal"), None),
        P(("slab", "deal")),
        P("slab", "deal"),
        P("slab", "deal", None, None),
        P("slab", "deal", None),
    )
    return jax.shard_map(
        body,
        mesh=mesh,
        in_specs=placed,
        out_specs=(
            P(("slab", "deal"), None, None),
            P("slab", "deal", None, None, None, None),
            P(None, "slab", "deal"),
        ),
        check_vma=False,
    )
```

```python
import functools

import jax
import jax.numpy as jnp
from jax import lax
from jax.experimental import pallas as pl
from jax.experimental.pallas import tpu as pltpu
from jax.sharding import PartitionSpec as P

PX = 64
PLANE = 8192
TILE = 256
LANES = 128
SPAN = 32

time_step = 0.1
viscosity = 0.2
gravity_pull = (3.0, 0.0, -5.0)

VMEM_LIMIT = 20 * 1024 * 1024
DEPOSIT_LIMIT = 60 * 1024 * 1024


def deposit_span(at, first, start, stop, ins, out_ref, shift, tiles_ref, parts_ref):
    off_ref, vel_ref, aff_ref, mass_ref, cell_ref = ins
    slots = lax.broadcasted_iota(jnp.int32, (LANES, LANES), 0).astype(jnp.float32)
    slots = slots.astype(jnp.bfloat16)
    one, zero = jnp.ones((), jnp.bfloat16), jnp.zeros((), jnp.bfloat16)
    spot = lax.broadcasted_iota(jnp.int32, (8, LANES), 0)
    sums = []
    for g in range(SPAN // 8):
        rows = pl.ds(pl.multiple_of(at + g * 8, 8), 8)
        offset = [off_ref[k, rows, :] for k in range(3)]
        block = first + at + g * 8 + spot
        w = jnp.where((block >= start) & (block < stop), mass_ref[rows, :], 0.0)
        values = []
        for k in range(3):
            m = vel_ref[k, rows, :]
            for j in range(3):
                m = m - aff_ref[3 * k + j, rows, :] * offset[j]
            values.append(w * m)
        values.append(w)
        c = cell_ref[rows, :]
        upper = c >= LANES
        base = g * LANES
        for k in range(4):
            high = values[k].astype(jnp.bfloat16).astype(jnp.float32)
            low = values[k] - high
            for s, part in enumerate((high, low)):
                put = base + s * 64 + k * 8
                parts_ref[put:put + 8, :] = jnp.where(upper, 0.0, part)
                parts_ref[put + 32:put + 40, :] = jnp.where(upper, part, 0.0)
        lane = (c & (LANES - 1)).astype(jnp.float32)
        for u in range(8):
            lhs = parts_ref[pl.ds(base + u, 16, stride=8), :].astype(jnp.bfloat16)
            row = jnp.broadcast_to(lane[u:u + 1], (16, LANES)).astype(jnp.bfloat16)
            select = jnp.where(jnp.concatenate([row] * 8, axis=0) == slots, one, zero)
            r = lax.dot_general(lhs, select, (((1,), (1,)), ((), ())),
                                preferred_element_type=jnp.float32)
            sums.append(r[:8] + r[8:])
    for u in range(SPAN):
        block = first + at + u
        t = tiles_ref[block] - shift
        inside = (block >= start) & (block < stop)
        out_ref[jnp.where(inside, t, 0)] += sums[u]


def first_at_least(tiles_ref, count, bound):
    found = 0
    for bit in reversed(range(count.bit_length())):
        far = found + (1 << bit)
        under = tiles_ref[jnp.minimum(far, count) - 1] < bound
        found = jnp.where((far <= count) & under, far, found)
    return found


def deposit_range(first, blocks, start, stop, ins, out_ref, shift, tiles_ref, parts_ref):
    low = lax.div(jnp.clip(start - first, 0, blocks), SPAN)
    high = lax.div(jnp.clip(stop - first, 0, blocks) + SPAN - 1, SPAN)
    high = jnp.where(stop > start, high, low)

    def step(i, carry):
        deposit_span(i * SPAN, first, start, stop, ins, out_ref, shift, tiles_ref, parts_ref)
        return carry

    lax.fori_loop(low, high, step, 0)


def chunk_specs(blocks, chunk, leads):
    def spec(lead):
        return pl.BlockSpec(lead + (blocks, LANES),
                            lambda i: (0,) * len(lead) + (chunk(i), 0))

    return [spec(lead) for lead in leads]


def deposit_kernel(facts_ref, tiles_ref, *refs, blocks, side, total, edges):
    ins, outs, (parts_ref, step_ref) = refs[:5], refs[5:-2], refs[-2:]
    nb = tiles_ref.shape[0]
    steps = nb // blocks
    base, live = facts_ref[3], facts_ref[4]
    low = jnp.minimum(first_at_least(tiles_ref, nb, base + side), live)
    high = jnp.minimum(first_at_least(tiles_ref, nb, base + total - side), live)
    for ref in outs:
        ref[...] = jnp.zeros_like(ref)
    step_ref[0] = 0

    def up_to(x):
        return lax.div(x + blocks - 1, blocks)

    if edges:
        head = up_to(low)
        tail = jnp.maximum(lax.div(high, blocks), head)
        needed = head + jnp.maximum(up_to(live) - tail, 0)
    else:
        head = 0
        tail = lax.div(low, blocks)
        needed = up_to(high) - tail

    def chunk(i):
        return jnp.clip(jnp.where(i < head, i, i - head + tail), 0, steps - 1)

    def work(*blocks_in):
        first = chunk(step_ref[0]) * blocks
        step_ref[0] = step_ref[0] + 1
        if edges:
            up_ref, down_ref = outs
            deposit_range(first, blocks, 0, low, blocks_in, up_ref, base, tiles_ref, parts_ref)
            deposit_range(first, blocks, high, live, blocks_in, down_ref, base + total - side,
                          tiles_ref, parts_ref)
        else:
            deposit_range(first, blocks, low, high, blocks_in, outs[0], base + side,
                          tiles_ref, parts_ref)

    pltpu.emit_pipeline(
        work, grid=(jnp.maximum(needed, 1),),
        in_specs=chunk_specs(blocks, chunk, ((3,), (3,), (9,), (), ())),
    )(*ins)


def update_kernel(facts_ref, tiles_ref, off_ref, cell_ref, settled_ref, out_ref,
                  picked_ref, step_ref, *, blocks):
    base = facts_ref[3]
    step_ref[0] = 0

    def work(off_ref, cell_ref, out_ref):
        first = step_ref[0] * blocks
        step_ref[0] = step_ref[0] + 1

        def step(i, carry):
            for g in range(SPAN // 8):
                rows = pl.ds(pl.multiple_of(i * SPAN + g * 8, 8), 8)
                c = cell_ref[rows, :]
                lane = c & (LANES - 1)
                at = g * 64
                for u in range(8):
                    tile = settled_ref[tiles_ref[first + i * SPAN + g * 8 + u] - base]
                    where = jnp.broadcast_to(lane[u:u + 1], (8, LANES))
                    put = at + u * 8
                    picked_ref[put:put + 8, :] = jnp.take_along_axis(tile, where, axis=1)
                offset = [off_ref[k, rows, :] for k in range(3)]
                for k in range(3):
                    v = jnp.where(c >= LANES, picked_ref[pl.ds(at + 4 + k, 8, stride=8), :],
                                  picked_ref[pl.ds(at + k, 8, stride=8), :])
                    out_ref[k, rows, :] = offset[k] + time_step * v
                    out_ref[3 + k, rows, :] = v
                    for j in range(3):
                        out_ref[6 + 3 * k + j, rows, :] = (-4.0 * v) * offset[j]
            return carry

        lax.fori_loop(0, blocks // SPAN, step, 0)

    pltpu.emit_pipeline(
        work, grid=(tiles_ref.shape[0] // blocks,),
        in_specs=chunk_specs(blocks, lambda i: i, ((3,), ())),
        out_specs=chunk_specs(blocks, lambda i: i, ((15,),)),
    )(off_ref, cell_ref, out_ref)


def grid_kernel(ends_ref, tiles_ref, lists_ref, counts_ref, up_ref, mid_ref, down_ref,
                before_ref, after_ref, off_hbm, mass_hbm, cell_hbm,
                settled_ref, *refs, row, margin, deals):
    *refs, off_ref, mass_ref, cell_ref, sems = refs
    *piece_refs, rec_down_ref, rec_up_ref, speed_ref = refs
    fetches = [pltpu.make_async_copy(a, b, sems.at[i]) for i, (a, b) in enumerate(
        ((off_hbm, off_ref), (mass_hbm, mass_ref), (cell_hbm, cell_ref)))]
    for fetch in fetches:
        fetch.start()
    rec_refs = (rec_down_ref, rec_up_ref)
    total = settled_ref.shape[0]
    side = before_ref.shape[0]
    inner = side - row
    rid = lax.broadcasted_iota(jnp.int32, (1, 8, LANES), 1)
    pull = jnp.zeros((1, 8, LANES), jnp.float32)
    for k in range(3):
        pull = jnp.where(rid % 4 == k, time_step * gravity_pull[k], pull)

    def speed_of(x):
        mass = jnp.where(rid < 4, x[:, 3:4, :], x[:, 7:8, :])
        return x / jnp.maximum(mass, 1.0) + pull

    chunk = 8
    keep_first = 1.0 - ends_ref[0].astype(jnp.float32)
    keep_last = 1.0 - ends_ref[1].astype(jnp.float32)
    far = row + total - side

    def middle(i, carry):
        at = i * chunk
        speed_ref[pl.ds(row + side + at, chunk)] = speed_of(mid_ref[pl.ds(at, chunk)])
        return carry

    lax.fori_loop(0, mid_ref.shape[0] // chunk, middle, 0)

    def outer(i, carry):
        at = i * chunk
        speed_ref[pl.ds(at, chunk)] = speed_of(before_ref[pl.ds(at, chunk)]) * keep_first
        speed_ref[pl.ds(side + at, chunk)] = speed_of(up_ref[pl.ds(inner + at, chunk)])
        speed_ref[pl.ds(far + at, chunk)] = speed_of(down_ref[pl.ds(at, chunk)])
        speed_ref[pl.ds(row + total + at, chunk)] = (
            speed_of(after_ref[pl.ds(inner + at, chunk)]) * keep_last)
        return carry

    lax.fori_loop(0, row // chunk, outer, 0)

    def seam(i, carry):
        at = i * chunk
        x = speed_of(up_ref[pl.ds(at, chunk)] + before_ref[pl.ds(row + at, chunk)])
        speed_ref[pl.ds(row + at, chunk)] = x * jnp.where(at < margin * row, keep_first, 1.0)
        y = speed_of(down_ref[pl.ds(row + at, chunk)] + after_ref[pl.ds(at, chunk)])
        past = at >= inner - margin * row
        speed_ref[pl.ds(far + row + at, chunk)] = y * jnp.where(past, keep_last, 1.0)
        return carry

    lax.fori_loop(0, inner // chunk, seam, 0)

    def smooth(i, carry):
        at = i * chunk
        s = speed_ref[pl.ds(row + at, chunk)]
        settled_ref[pl.ds(at, chunk)] = s + viscosity * (
            speed_ref[pl.ds(2 * row + at, chunk)] + speed_ref[pl.ds(at, chunk)] - 2.0 * s)
        return carry

    lax.fori_loop(0, total // chunk, smooth, 0)

    flat = settled_ref.reshape(total * 8, LANES)
    planes = piece_refs[0].shape[1]
    across = row // deals
    for turn in range(deals):
        piece_ref = piece_refs[turn]
        corner = lax.rem(ends_ref[2] + turn, deals) * across

        def column(tc, carry, piece_ref=piece_ref, corner=corner):
            for group in range(planes // 8):
                for h in range(2):
                    for k in range(3):
                        start = (margin + group * 8) * row * 8 + (corner + tc) * 8 + h * 4 + k
                        x = flat[pl.ds(start, 8, stride=row * 8), :]
                        at = pl.multiple_of(tc * TILE + h * LANES, LANES)
                        piece_ref[k, group * 8:group * 8 + 8, pl.ds(at, LANES)] = x
            return carry

        lax.fori_loop(0, across, column, 0)

    for fetch in fetches:
        fetch.wait()
    slots = lists_ref.shape[1]

    def record(i, carry):
        for way in range(2):
            b = lists_ref[way, i]
            keep = jnp.where(i < counts_ref[way], 1.0, 0.0)
            c = cell_ref[pl.ds(b, 1), :]
            tile = settled_ref[tiles_ref[b] - ends_ref[3]]
            lane = jnp.broadcast_to(c & (LANES - 1), (8, LANES))
            g = jnp.take_along_axis(tile, lane, axis=1)
            v = jnp.where(c >= LANES, g[4:7], g[0:3])
            rec_ref = rec_refs[way]
            for k in range(3):
                o = off_ref[k, pl.ds(b, 1), :]
                rec_ref[i, k:k + 1, :] = (o + time_step * v[k:k + 1]) * keep
                rec_ref[i, pl.ds(6 + k, 3, stride=3), :] = ((-4.0 * v) * o) * keep
            rec_ref[i, 3:6, :] = v * keep
            rec_ref[i, 15:16, :] = mass_ref[pl.ds(b, 1), :] * keep
        return carry

    lax.fori_loop(0, slots, record, 0)


def assemble_kernel(facts_ref, *refs, deals):
    *piece_refs, left_ref, right_ref, grid_ref, arrivals_ref, sems = refs
    planes = piece_refs[0].shape[1]
    copies = []
    for turn, piece_ref in enumerate(piece_refs):
        slot = lax.rem(facts_ref[2] - turn + deals, deals)
        rows = pl.ds(pl.multiple_of(slot * planes, 8), planes)
        copies.append((piece_ref, grid_ref.at[:, rows, :]))
    copies.append((left_ref, arrivals_ref.at[0]))
    copies.append((right_ref, arrivals_ref.at[1]))
    started = [pltpu.make_async_copy(a, b, sems.at[i]) for i, (a, b) in enumerate(copies)]
    for c in started:
        c.start()
    for c in started:
        c.wait()


def body(offsets, velocity, affine, particle_mass, cell_in_tile, block_tile, live_blocks,
         send_lists, send_counts):
    axes = ("slab", "deal")
    slabs, deals = lax.axis_size("slab"), lax.axis_size("deal")
    count = slabs * deals
    slab, deal = lax.axis_index("slab"), lax.axis_index("deal")
    nb = offsets.shape[0]
    row = PLANE // TILE
    planes = PX // deals
    share = planes * row
    margin = -(-max(share // 16, 1) // row)
    total = (planes + 2 * margin) * row
    side = (2 * margin + 1) * row
    f32 = jnp.float32

    place = slab * deals + deal
    facts = jnp.stack([(place == 0).astype(jnp.int32), (place == count - 1).astype(jnp.int32),
                       deal, deal * share - margin * row, live_blocks[0, 0]])
    mig = send_lists.shape[-1]
    tiles = block_tile
    offsets, velocity, affine = (jnp.transpose(x, (1, 0, 2)) for x in (offsets, velocity, affine))
    blocks = 128 if nb % 128 == 0 else nb
    params = pltpu.CompilerParams(vmem_limit_bytes=VMEM_LIMIT)
    smem = pl.BlockSpec(memory_space=pltpu.SMEM)
    vmem = pl.BlockSpec(memory_space=pltpu.VMEM)
    hbm = pl.BlockSpec(memory_space=pltpu.HBM)
    counter = pltpu.SMEM((1,), jnp.int32)

    def deposit(edges, sizes, name):
        return pl.pallas_call(
            functools.partial(deposit_kernel, blocks=blocks, side=side, total=total, edges=edges),
            in_specs=[smem, smem] + [hbm] * 5,
            out_specs=[vmem] * len(sizes),
            out_shape=[jax.ShapeDtypeStruct((n, 8, LANES), f32) for n in sizes],
            scratch_shapes=[pltpu.VMEM((SPAN * 16, LANES), f32), counter],
            compiler_params=pltpu.CompilerParams(vmem_limit_bytes=DEPOSIT_LIMIT),
            cost_estimate=pl.CostEstimate(flops=nb * 16 * LANES * LANES, transcendentals=0,
                                          bytes_accessed=nb * 17 * LANES * 4),
            name=name,
        )(facts, tiles, offsets, velocity, affine, particle_mass, cell_in_tile)

    up, down = deposit(True, (side, side), "deposit_edges")
    before = lax.ppermute(down, axes, [(i, i + 1) for i in range(count - 1)])
    after = lax.ppermute(up, axes, [(i + 1, i) for i in range(count - 1)])
    mid, = deposit(False, (total - 2 * side,), "deposit_middle")

    width = PLANE // deals
    outs = ([jax.ShapeDtypeStruct((total, 8, LANES), f32)]
            + [jax.ShapeDtypeStruct((3, planes, width), f32)] * deals
            + [jax.ShapeDtypeStruct((mig, 16, LANES), f32)] * 2)
    settled, *pieces, leave_down, leave_up = pl.pallas_call(
        functools.partial(grid_kernel, row=row, margin=margin, deals=deals),
        in_specs=[smem] * 4 + [vmem] * 5 + [hbm] * 3,
        out_specs=[vmem] * len(outs),
        out_shape=outs,
        scratch_shapes=[pltpu.VMEM((total + 2 * row, 8, LANES), f32),
                        pltpu.VMEM((3, nb, LANES), f32), pltpu.VMEM((nb, LANES), f32),
                        pltpu.VMEM((nb, LANES), jnp.int32), pltpu.SemaphoreType.DMA((3,))],
        compiler_params=params,
        name="grid_step",
    )(facts, tiles, send_lists[0, 0], send_counts.reshape(2), up, mid, down, before, after,
      offsets, particle_mass, cell_in_tile)

    for k in range(1, deals):
        pairs = [(i, (i + k) % deals) for i in range(deals)]
        pieces[k] = lax.ppermute(pieces[k], "deal", pairs)
    from_left = lax.ppermute(leave_down, "slab", [(i, i + 1) for i in range(slabs - 1)])
    from_right = lax.ppermute(leave_up, "slab", [(i + 1, i) for i in range(slabs - 1)])

    state = pl.pallas_call(
        functools.partial(update_kernel, blocks=blocks),
        in_specs=[smem, smem, hbm, hbm, vmem],
        out_specs=hbm,
        out_shape=jax.ShapeDtypeStruct((15, nb, LANES), f32),
        scratch_shapes=[pltpu.VMEM((SPAN * 8, LANES), f32), counter],
        compiler_params=params,
        cost_estimate=pl.CostEstimate(flops=nb * 15 * LANES * 4,
                                      bytes_accessed=nb * 20 * LANES * 4, transcendentals=0),
        name="update",
    )(facts, tiles, offsets, cell_in_tile, settled)
    state = jnp.transpose(state, (1, 0, 2))

    anywhere = pl.BlockSpec(memory_space=pl.ANY)
    grid, arrivals = pl.pallas_call(
        functools.partial(assemble_kernel, deals=deals),
        in_specs=[smem] + [anywhere] * (deals + 2),
        out_specs=[anywhere] * 2,
        out_shape=[jax.ShapeDtypeStruct((3, PX, width), f32),
                   jax.ShapeDtypeStruct((2, mig, 16, LANES), f32)],
        scratch_shapes=[pltpu.SemaphoreType.DMA((deals + 2,))],
        compiler_params=pltpu.CompilerParams(vmem_limit_bytes=VMEM_LIMIT),
        name="assemble",
    )(facts, *pieces, from_left, from_right)
    arrivals = arrivals[None, None]
    return state, arrivals, grid


def solution(mesh):
    placed = (
        P(("slab", "deal"), None, None),
        P(("slab", "deal"), None, None),
        P(("slab", "deal"), None, None),
        P(("slab", "deal"), None),
        P(("slab", "deal"), None),
        P(("slab", "deal")),
        P("slab", "deal"),
        P("slab", "deal", None, None),
        P("slab", "deal", None),
    )
    return jax.shard_map(
        body,
        mesh=mesh,
        in_specs=placed,
        out_specs=(
            P(("slab", "deal"), None, None),
            P("slab", "deal", None, None, None, None),
            P(None, "slab", "deal"),
        ),
        check_vma=False,
    )
```

```python
import functools

import jax
import jax.numpy as jnp
from jax import lax
from jax.experimental import pallas as pl
from jax.experimental.pallas import tpu as pltpu
from jax.sharding import PartitionSpec as P

PX = 64
PLANE = 8192
TILE = 256
LANES = 128
SPAN = 32
WIDE_SPAN = 64

time_step = 0.1
viscosity = 0.2
gravity_pull = (3.0, 0.0, -5.0)

VMEM_LIMIT = 20 * 1024 * 1024
DEPOSIT_LIMIT = 60 * 1024 * 1024


def deposit_span(at, first, start, stop, ins, out_ref, shift, tiles_ref, parts_ref):
    off_ref, vel_ref, aff_ref, mass_ref, cell_ref = ins
    slots = lax.broadcasted_iota(jnp.int32, (LANES, LANES), 0).astype(jnp.float32)
    slots = slots.astype(jnp.bfloat16)
    one, zero = jnp.ones((), jnp.bfloat16), jnp.zeros((), jnp.bfloat16)
    blank = jnp.zeros((16, LANES), jnp.bfloat16)
    spot = lax.broadcasted_iota(jnp.int32, (8, LANES), 0)
    sums = []
    for g in range(SPAN // 8):
        rows = pl.ds(pl.multiple_of(at + g * 8, 8), 8)
        offset = [off_ref[k, rows, :] for k in range(3)]
        block = first + at + g * 8 + spot
        w = jnp.where((block >= start) & (block < stop), mass_ref[rows, :], 0.0)
        values = []
        for k in range(3):
            m = vel_ref[k, rows, :]
            for j in range(3):
                m = m - aff_ref[3 * k + j, rows, :] * offset[j]
            values.append(w * m)
        values.append(w)
        c = cell_ref[rows, :]
        upper = c >= LANES
        base = g * LANES
        for k in range(4):
            high = values[k].astype(jnp.bfloat16).astype(jnp.float32)
            low = values[k] - high
            for s, part in enumerate((high, low)):
                put = base + s * 64 + k * 8
                parts_ref[put:put + 8, :] = jnp.where(upper, 0.0, part)
                parts_ref[put + 32:put + 40, :] = jnp.where(upper, part, 0.0)
        lane = (c & (LANES - 1)).astype(jnp.float32)
        lefts, selects = [], []
        for u in range(8):
            lefts.append(parts_ref[pl.ds(base + u, 16, stride=8), :].astype(jnp.bfloat16))
            row = jnp.broadcast_to(lane[u:u + 1], (16, LANES)).astype(jnp.bfloat16)
            selects.append(jnp.where(jnp.concatenate([row] * 8, axis=0) == slots, one, zero))
        for u in range(0, 8, 2):
            lhs = jnp.concatenate([jnp.concatenate([lefts[u], blank], axis=1),
                                   jnp.concatenate([blank, lefts[u + 1]], axis=1)], axis=0)
            select = jnp.concatenate([selects[u], selects[u + 1]], axis=1)
            r = lax.dot_general(lhs, select, (((1,), (1,)), ((), ())),
                                preferred_element_type=jnp.float32)
            sums.append(r[:8] + r[8:16])
            sums.append(r[16:24] + r[24:])
    for u in range(SPAN):
        block = first + at + u
        t = tiles_ref[block] - shift
        inside = (block >= start) & (block < stop)
        out_ref[jnp.where(inside, t, 0)] += sums[u]


def first_at_least(tiles_ref, count, bound):
    found = 0
    for bit in reversed(range(count.bit_length())):
        far = found + (1 << bit)
        under = tiles_ref[jnp.minimum(far, count) - 1] < bound
        found = jnp.where((far <= count) & under, far, found)
    return found


def deposit_range(first, blocks, start, stop, ins, out_ref, shift, tiles_ref, parts_ref):
    low = lax.div(jnp.clip(start - first, 0, blocks), SPAN)
    high = lax.div(jnp.clip(stop - first, 0, blocks) + SPAN - 1, SPAN)
    high = jnp.where(stop > start, high, low)

    def step(i, carry):
        deposit_span(i * SPAN, first, start, stop, ins, out_ref, shift, tiles_ref, parts_ref)
        return carry

    lax.fori_loop(low, high, step, 0)


def chunk_specs(blocks, chunk, leads):
    def spec(lead):
        return pl.BlockSpec(lead + (blocks, LANES),
                            lambda i: (0,) * len(lead) + (chunk(i), 0))

    return [spec(lead) for lead in leads]


def deposit_kernel(facts_ref, tiles_ref, *refs, blocks, side, total, edges):
    ins, outs, (parts_ref, step_ref) = refs[:5], refs[5:-2], refs[-2:]
    nb = tiles_ref.shape[0]
    steps = nb // blocks
    base, live = facts_ref[3], facts_ref[4]
    low = jnp.minimum(first_at_least(tiles_ref, nb, base + side), live)
    high = jnp.minimum(first_at_least(tiles_ref, nb, base + total - side), live)
    for ref in outs:
        ref[...] = jnp.zeros_like(ref)
    step_ref[0] = 0

    def up_to(x):
        return lax.div(x + blocks - 1, blocks)

    if edges:
        head = up_to(low)
        tail = jnp.maximum(lax.div(high, blocks), head)
        needed = head + jnp.maximum(up_to(live) - tail, 0)
    else:
        head = 0
        tail = lax.div(low, blocks)
        needed = up_to(high) - tail

    def chunk(i):
        return jnp.clip(jnp.where(i < head, i, i - head + tail), 0, steps - 1)

    def work(*blocks_in):
        first = chunk(step_ref[0]) * blocks
        step_ref[0] = step_ref[0] + 1
        if edges:
            up_ref, down_ref = outs
            deposit_range(first, blocks, 0, low, blocks_in, up_ref, base, tiles_ref, parts_ref)
            deposit_range(first, blocks, high, live, blocks_in, down_ref, base + total - side,
                          tiles_ref, parts_ref)
        else:
            deposit_range(first, blocks, low, high, blocks_in, outs[0], base + side,
                          tiles_ref, parts_ref)

    pltpu.emit_pipeline(
        work, grid=(jnp.maximum(needed, 1),),
        in_specs=chunk_specs(blocks, chunk, ((3,), (3,), (9,), (), ())),
    )(*ins)


def update_kernel(facts_ref, tiles_ref, off_ref, cell_ref, settled_ref, out_ref,
                  picked_ref, step_ref, *, blocks):
    base = facts_ref[3]
    step_ref[0] = 0

    def work(off_ref, cell_ref, out_ref):
        first = step_ref[0] * blocks
        step_ref[0] = step_ref[0] + 1

        def step(i, carry):
            for g in range(WIDE_SPAN // 8):
                rows = pl.ds(pl.multiple_of(i * WIDE_SPAN + g * 8, 8), 8)
                c = cell_ref[rows, :]
                lane = c & (LANES - 1)
                at = g * 64
                for u in range(8):
                    tile = settled_ref[tiles_ref[first + i * WIDE_SPAN + g * 8 + u] - base]
                    where = jnp.broadcast_to(lane[u:u + 1], (8, LANES))
                    put = at + u * 8
                    picked_ref[put:put + 8, :] = jnp.take_along_axis(tile, where, axis=1)
                offset = [off_ref[k, rows, :] for k in range(3)]
                for k in range(3):
                    v = jnp.where(c >= LANES, picked_ref[pl.ds(at + 4 + k, 8, stride=8), :],
                                  picked_ref[pl.ds(at + k, 8, stride=8), :])
                    out_ref[k, rows, :] = offset[k] + time_step * v
                    out_ref[3 + k, rows, :] = v
                    for j in range(3):
                        out_ref[6 + 3 * k + j, rows, :] = (-4.0 * v) * offset[j]
            return carry

        lax.fori_loop(0, blocks // WIDE_SPAN, step, 0)

    pltpu.emit_pipeline(
        work, grid=(tiles_ref.shape[0] // blocks,),
        in_specs=chunk_specs(blocks, lambda i: i, ((3,), ())),
        out_specs=chunk_specs(blocks, lambda i: i, ((15,),)),
    )(off_ref, cell_ref, out_ref)


def grid_kernel(ends_ref, tiles_ref, lists_ref, counts_ref, up_ref, mid_ref, down_ref,
                before_ref, after_ref, off_hbm, mass_hbm, cell_hbm,
                settled_ref, *refs, row, margin, deals):
    *refs, off_ref, mass_ref, cell_ref, sems = refs
    *piece_refs, rec_down_ref, rec_up_ref, speed_ref = refs
    fetches = [pltpu.make_async_copy(a, b, sems.at[i]) for i, (a, b) in enumerate(
        ((off_hbm, off_ref), (mass_hbm, mass_ref), (cell_hbm, cell_ref)))]
    for fetch in fetches:
        fetch.start()
    rec_refs = (rec_down_ref, rec_up_ref)
    total = settled_ref.shape[0]
    side = before_ref.shape[0]
    inner = side - row
    rid = lax.broadcasted_iota(jnp.int32, (1, 8, LANES), 1)
    pull = jnp.zeros((1, 8, LANES), jnp.float32)
    for k in range(3):
        pull = jnp.where(rid % 4 == k, time_step * gravity_pull[k], pull)

    def speed_of(x):
        mass = jnp.where(rid < 4, x[:, 3:4, :], x[:, 7:8, :])
        return x / jnp.maximum(mass, 1.0) + pull

    chunk = 16
    keep_first = 1.0 - ends_ref[0].astype(jnp.float32)
    keep_last = 1.0 - ends_ref[1].astype(jnp.float32)
    far = row + total - side

    def middle(i, carry):
        at = i * chunk
        speed_ref[pl.ds(row + side + at, chunk)] = speed_of(mid_ref[pl.ds(at, chunk)])
        return carry

    lax.fori_loop(0, mid_ref.shape[0] // chunk, middle, 0)

    def outer(i, carry):
        at = i * chunk
        speed_ref[pl.ds(at, chunk)] = speed_of(before_ref[pl.ds(at, chunk)]) * keep_first
        speed_ref[pl.ds(side + at, chunk)] = speed_of(up_ref[pl.ds(inner + at, chunk)])
        speed_ref[pl.ds(far + at, chunk)] = speed_of(down_ref[pl.ds(at, chunk)])
        speed_ref[pl.ds(row + total + at, chunk)] = (
            speed_of(after_ref[pl.ds(inner + at, chunk)]) * keep_last)
        return carry

    lax.fori_loop(0, row // chunk, outer, 0)

    def seam(i, carry):
        at = i * chunk
        x = speed_of(up_ref[pl.ds(at, chunk)] + before_ref[pl.ds(row + at, chunk)])
        speed_ref[pl.ds(row + at, chunk)] = x * jnp.where(at < margin * row, keep_first, 1.0)
        y = speed_of(down_ref[pl.ds(row + at, chunk)] + after_ref[pl.ds(at, chunk)])
        past = at >= inner - margin * row
        speed_ref[pl.ds(far + row + at, chunk)] = y * jnp.where(past, keep_last, 1.0)
        return carry

    lax.fori_loop(0, inner // chunk, seam, 0)

    def smooth(i, carry):
        at = i * chunk
        s = speed_ref[pl.ds(row + at, chunk)]
        settled_ref[pl.ds(at, chunk)] = s + viscosity * (
            speed_ref[pl.ds(2 * row + at, chunk)] + speed_ref[pl.ds(at, chunk)] - 2.0 * s)
        return carry

    lax.fori_loop(0, total // chunk, smooth, 0)

    flat = settled_ref.reshape(total * 8, LANES)
    planes = piece_refs[0].shape[1]
    across = row // deals
    for turn in range(deals):
        piece_ref = piece_refs[turn]
        corner = lax.rem(ends_ref[2] + turn, deals) * across

        def column(tc, carry, piece_ref=piece_ref, corner=corner):
            for group in range(planes // 8):
                for h in range(2):
                    for k in range(3):
                        start = (margin + group * 8) * row * 8 + (corner + tc) * 8 + h * 4 + k
                        x = flat[pl.ds(start, 8, stride=row * 8), :]
                        at = pl.multiple_of(tc * TILE + h * LANES, LANES)
                        piece_ref[k, group * 8:group * 8 + 8, pl.ds(at, LANES)] = x
            return carry

        lax.fori_loop(0, across, column, 0)

    for fetch in fetches:
        fetch.wait()
    slots = lists_ref.shape[1]

    def record(i, carry):
        for way in range(2):
            b = lists_ref[way, i]
            keep = jnp.where(i < counts_ref[way], 1.0, 0.0)
            c = cell_ref[pl.ds(b, 1), :]
            tile = settled_ref[tiles_ref[b] - ends_ref[3]]
            lane = jnp.broadcast_to(c & (LANES - 1), (8, LANES))
            g = jnp.take_along_axis(tile, lane, axis=1)
            v = jnp.where(c >= LANES, g[4:7], g[0:3])
            rec_ref = rec_refs[way]
            for k in range(3):
                o = off_ref[k, pl.ds(b, 1), :]
                rec_ref[i, k:k + 1, :] = (o + time_step * v[k:k + 1]) * keep
                rec_ref[i, pl.ds(6 + k, 3, stride=3), :] = ((-4.0 * v) * o) * keep
            rec_ref[i, 3:6, :] = v * keep
            rec_ref[i, 15:16, :] = mass_ref[pl.ds(b, 1), :] * keep
        return carry

    lax.fori_loop(0, slots, record, 0)


def assemble_kernel(facts_ref, *refs, deals):
    *piece_refs, left_ref, right_ref, grid_ref, arrivals_ref, sems = refs
    planes = piece_refs[0].shape[1]
    copies = []
    for turn, piece_ref in enumerate(piece_refs):
        slot = lax.rem(facts_ref[2] - turn + deals, deals)
        rows = pl.ds(pl.multiple_of(slot * planes, 8), planes)
        copies.append((piece_ref, grid_ref.at[:, rows, :]))
    copies.append((left_ref, arrivals_ref.at[0]))
    copies.append((right_ref, arrivals_ref.at[1]))
    started = [pltpu.make_async_copy(a, b, sems.at[i]) for i, (a, b) in enumerate(copies)]
    for c in started:
        c.start()
    for c in started:
        c.wait()


def body(offsets, velocity, affine, particle_mass, cell_in_tile, block_tile, live_blocks,
         send_lists, send_counts):
    axes = ("slab", "deal")
    slabs, deals = lax.axis_size("slab"), lax.axis_size("deal")
    count = slabs * deals
    slab, deal = lax.axis_index("slab"), lax.axis_index("deal")
    nb = offsets.shape[0]
    row = PLANE // TILE
    planes = PX // deals
    share = planes * row
    margin = -(-max(share // 16, 1) // row)
    total = (planes + 2 * margin) * row
    side = (2 * margin + 1) * row
    f32 = jnp.float32

    place = slab * deals + deal
    facts = jnp.stack([(place == 0).astype(jnp.int32), (place == count - 1).astype(jnp.int32),
                       deal, deal * share - margin * row, live_blocks[0, 0]])
    mig = send_lists.shape[-1]
    tiles = block_tile
    offsets, velocity, affine = (jnp.transpose(x, (1, 0, 2)) for x in (offsets, velocity, affine))
    blocks = 128 if nb % 128 == 0 else nb
    params = pltpu.CompilerParams(vmem_limit_bytes=VMEM_LIMIT)
    smem = pl.BlockSpec(memory_space=pltpu.SMEM)
    vmem = pl.BlockSpec(memory_space=pltpu.VMEM)
    hbm = pl.BlockSpec(memory_space=pltpu.HBM)
    counter = pltpu.SMEM((1,), jnp.int32)

    def deposit(edges, sizes, name):
        return pl.pallas_call(
            functools.partial(deposit_kernel, blocks=blocks, side=side, total=total, edges=edges),
            in_specs=[smem, smem] + [hbm] * 5,
            out_specs=[vmem] * len(sizes),
            out_shape=[jax.ShapeDtypeStruct((n, 8, LANES), f32) for n in sizes],
            scratch_shapes=[pltpu.VMEM((SPAN * 16, LANES), f32), counter],
            compiler_params=pltpu.CompilerParams(vmem_limit_bytes=DEPOSIT_LIMIT),
            cost_estimate=pl.CostEstimate(flops=nb * 16 * LANES * LANES, transcendentals=0,
                                          bytes_accessed=nb * 17 * LANES * 4),
            name=name,
        )(facts, tiles, offsets, velocity, affine, particle_mass, cell_in_tile)

    up, down = deposit(True, (side, side), "deposit_edges")
    before = lax.ppermute(down, axes, [(i, i + 1) for i in range(count - 1)])
    after = lax.ppermute(up, axes, [(i + 1, i) for i in range(count - 1)])
    mid, = deposit(False, (total - 2 * side,), "deposit_middle")

    width = PLANE // deals
    outs = ([jax.ShapeDtypeStruct((total, 8, LANES), f32)]
            + [jax.ShapeDtypeStruct((3, planes, width), f32)] * deals
            + [jax.ShapeDtypeStruct((mig, 16, LANES), f32)] * 2)
    settled, *pieces, leave_down, leave_up = pl.pallas_call(
        functools.partial(grid_kernel, row=row, margin=margin, deals=deals),
        in_specs=[smem] * 4 + [vmem] * 5 + [hbm] * 3,
        out_specs=[vmem] * len(outs),
        out_shape=outs,
        scratch_shapes=[pltpu.VMEM((total + 2 * row, 8, LANES), f32),
                        pltpu.VMEM((3, nb, LANES), f32), pltpu.VMEM((nb, LANES), f32),
                        pltpu.VMEM((nb, LANES), jnp.int32), pltpu.SemaphoreType.DMA((3,))],
        compiler_params=params,
        name="grid_step",
    )(facts, tiles, send_lists[0, 0], send_counts.reshape(2), up, mid, down, before, after,
      offsets, particle_mass, cell_in_tile)

    for k in range(1, deals):
        pairs = [(i, (i + k) % deals) for i in range(deals)]
        pieces[k] = lax.ppermute(pieces[k], "deal", pairs)
    from_left = lax.ppermute(leave_down, "slab", [(i, i + 1) for i in range(slabs - 1)])
    from_right = lax.ppermute(leave_up, "slab", [(i + 1, i) for i in range(slabs - 1)])

    state = pl.pallas_call(
        functools.partial(update_kernel, blocks=blocks),
        in_specs=[smem, smem, hbm, hbm, vmem],
        out_specs=hbm,
        out_shape=jax.ShapeDtypeStruct((15, nb, LANES), f32),
        scratch_shapes=[pltpu.VMEM((WIDE_SPAN * 8, LANES), f32), counter],
        compiler_params=params,
        cost_estimate=pl.CostEstimate(flops=nb * 15 * LANES * 4,
                                      bytes_accessed=nb * 20 * LANES * 4, transcendentals=0),
        name="update",
    )(facts, tiles, offsets, cell_in_tile, settled)
    state = jnp.transpose(state, (1, 0, 2))

    anywhere = pl.BlockSpec(memory_space=pl.ANY)
    grid, arrivals = pl.pallas_call(
        functools.partial(assemble_kernel, deals=deals),
        in_specs=[smem] + [anywhere] * (deals + 2),
        out_specs=[anywhere] * 2,
        out_shape=[jax.ShapeDtypeStruct((3, PX, width), f32),
                   jax.ShapeDtypeStruct((2, mig, 16, LANES), f32)],
        scratch_shapes=[pltpu.SemaphoreType.DMA((deals + 2,))],
        compiler_params=pltpu.CompilerParams(vmem_limit_bytes=VMEM_LIMIT),
        name="assemble",
    )(facts, *pieces, from_left, from_right)
    arrivals = arrivals[None, None]
    return state, arrivals, grid


def solution(mesh):
    placed = (
        P(("slab", "deal"), None, None),
        P(("slab", "deal"), None, None),
        P(("slab", "deal"), None, None),
        P(("slab", "deal"), None),
        P(("slab", "deal"), None),
        P(("slab", "deal")),
        P("slab", "deal"),
        P("slab", "deal", None, None),
        P("slab", "deal", None),
    )
    return jax.shard_map(
        body,
        mesh=mesh,
        in_specs=placed,
        out_specs=(
            P(("slab", "deal"), None, None),
            P("slab", "deal", None, None, None, None),
            P(None, "slab", "deal"),
        ),
        check_vma=False,
    )
```

```python
import functools
import math

import jax
import jax.numpy as jnp
from jax import lax
from jax.experimental import pallas as pl
from jax.experimental.pallas import tpu as pltpu
from jax.sharding import PartitionSpec as P

PX = 64
PLANE = 8192
TILE = 256
LANES = 128
SPAN = 32
WIDE_SPAN = 64

time_step = 0.1
viscosity = 0.2
gravity_pull = (3.0, 0.0, -5.0)

VMEM_LIMIT = 20 * 1024 * 1024
DEPOSIT_LIMIT = 60 * 1024 * 1024


def deposit_span(at, first, start, stop, ins, out_ref, shift, tiles_ref, parts_ref):
    off_ref, vel_ref, aff_ref, mass_ref, cell_ref = ins
    slots = lax.broadcasted_iota(jnp.int32, (LANES, LANES), 0).astype(jnp.float32)
    slots = slots.astype(jnp.bfloat16)
    one, zero = jnp.ones((), jnp.bfloat16), jnp.zeros((), jnp.bfloat16)
    blank = jnp.zeros((16, LANES), jnp.bfloat16)
    spot = lax.broadcasted_iota(jnp.int32, (8, LANES), 0)
    sums = []
    for g in range(SPAN // 8):
        rows = pl.ds(pl.multiple_of(at + g * 8, 8), 8)
        offset = [off_ref[k, rows, :] for k in range(3)]
        block = first + at + g * 8 + spot
        w = jnp.where((block >= start) & (block < stop), mass_ref[rows, :], 0.0)
        values = []
        for k in range(3):
            m = vel_ref[k, rows, :]
            for j in range(3):
                m = m - aff_ref[3 * k + j, rows, :] * offset[j]
            values.append(w * m)
        values.append(w)
        c = cell_ref[rows, :]
        upper = c >= LANES
        base = g * LANES
        for k in range(4):
            high = values[k].astype(jnp.bfloat16).astype(jnp.float32)
            low = values[k] - high
            for s, part in enumerate((high, low)):
                put = base + s * 64 + k * 8
                parts_ref[put:put + 8, :] = jnp.where(upper, 0.0, part)
                parts_ref[put + 32:put + 40, :] = jnp.where(upper, part, 0.0)
        lane = (c & (LANES - 1)).astype(jnp.float32)
        lefts, selects = [], []
        for u in range(8):
            lefts.append(parts_ref[pl.ds(base + u, 16, stride=8), :].astype(jnp.bfloat16))
            row = jnp.broadcast_to(lane[u:u + 1], (16, LANES)).astype(jnp.bfloat16)
            selects.append(jnp.where(jnp.concatenate([row] * 8, axis=0) == slots, one, zero))
        for u in range(0, 8, 2):
            lhs = jnp.concatenate([jnp.concatenate([lefts[u], blank], axis=1),
                                   jnp.concatenate([blank, lefts[u + 1]], axis=1)], axis=0)
            select = jnp.concatenate([selects[u], selects[u + 1]], axis=1)
            r = lax.dot_general(lhs, select, (((1,), (1,)), ((), ())),
                                preferred_element_type=jnp.float32)
            sums.append(r[:8] + r[8:16])
            sums.append(r[16:24] + r[24:])
    for u in range(SPAN):
        block = first + at + u
        t = tiles_ref[block] - shift
        inside = (block >= start) & (block < stop)
        out_ref[jnp.where(inside, t, 0)] += sums[u]


def first_at_least(tiles_ref, count, bound):
    found = 0
    for bit in reversed(range(count.bit_length())):
        far = found + (1 << bit)
        under = tiles_ref[jnp.minimum(far, count) - 1] < bound
        found = jnp.where((far <= count) & under, far, found)
    return found


def deposit_range(first, blocks, start, stop, ins, out_ref, shift, tiles_ref, parts_ref):
    low = lax.div(jnp.clip(start - first, 0, blocks), SPAN)
    high = lax.div(jnp.clip(stop - first, 0, blocks) + SPAN - 1, SPAN)
    high = jnp.where(stop > start, high, low)

    def step(i, carry):
        deposit_span(i * SPAN, first, start, stop, ins, out_ref, shift, tiles_ref, parts_ref)
        return carry

    lax.fori_loop(low, high, step, 0)


def chunk_specs(blocks, chunk, leads):
    def spec(lead):
        return pl.BlockSpec(lead + (blocks, LANES),
                            lambda i: (0,) * len(lead) + (chunk(i), 0))

    return [spec(lead) for lead in leads]


def deposit_kernel(facts_ref, tiles_ref, *refs, blocks, side, total, edges):
    ins, outs, (parts_ref, step_ref) = refs[:5], refs[5:-2], refs[-2:]
    nb = tiles_ref.shape[0]
    steps = nb // blocks
    base, live = facts_ref[3], facts_ref[4]
    low = jnp.minimum(first_at_least(tiles_ref, nb, base + side), live)
    high = jnp.minimum(first_at_least(tiles_ref, nb, base + total - side), live)
    for ref in outs:
        ref[...] = jnp.zeros_like(ref)
    step_ref[0] = 0

    def up_to(x):
        return lax.div(x + blocks - 1, blocks)

    if edges:
        head = up_to(low)
        tail = jnp.maximum(lax.div(high, blocks), head)
        needed = head + jnp.maximum(up_to(live) - tail, 0)
    else:
        head = 0
        tail = lax.div(low, blocks)
        needed = up_to(high) - tail

    def chunk(i):
        return jnp.clip(jnp.where(i < head, i, i - head + tail), 0, steps - 1)

    def work(*blocks_in):
        first = chunk(step_ref[0]) * blocks
        step_ref[0] = step_ref[0] + 1
        if edges:
            up_ref, down_ref = outs
            deposit_range(first, blocks, 0, low, blocks_in, up_ref, base, tiles_ref, parts_ref)
            deposit_range(first, blocks, high, live, blocks_in, down_ref, base + total - side,
                          tiles_ref, parts_ref)
        else:
            deposit_range(first, blocks, low, high, blocks_in, outs[0], base + side,
                          tiles_ref, parts_ref)

    pltpu.emit_pipeline(
        work, grid=(jnp.maximum(needed, 1),),
        in_specs=chunk_specs(blocks, chunk, ((3,), (3,), (9,), (), ())),
    )(*ins)


def update_kernel(facts_ref, tiles_ref, off_ref, cell_ref, settled_ref, out_ref,
                  picked_ref, step_ref, *, blocks):
    base = facts_ref[3]
    step_ref[0] = 0

    def work(off_ref, cell_ref, out_ref):
        first = step_ref[0] * blocks
        step_ref[0] = step_ref[0] + 1

        def step(i, carry):
            for g in range(WIDE_SPAN // 8):
                rows = pl.ds(pl.multiple_of(i * WIDE_SPAN + g * 8, 8), 8)
                c = cell_ref[rows, :]
                lane = c & (LANES - 1)
                at = g * 64
                for u in range(8):
                    tile = settled_ref[tiles_ref[first + i * WIDE_SPAN + g * 8 + u] - base]
                    where = jnp.broadcast_to(lane[u:u + 1], (8, LANES))
                    put = at + u * 8
                    picked_ref[put:put + 8, :] = jnp.take_along_axis(tile, where, axis=1)
                offset = [off_ref[k, rows, :] for k in range(3)]
                for k in range(3):
                    v = jnp.where(c >= LANES, picked_ref[pl.ds(at + 4 + k, 8, stride=8), :],
                                  picked_ref[pl.ds(at + k, 8, stride=8), :])
                    out_ref[k, rows, :] = offset[k] + time_step * v
                    out_ref[3 + k, rows, :] = v
                    for j in range(3):
                        out_ref[6 + 3 * k + j, rows, :] = (-4.0 * v) * offset[j]
            return carry

        lax.fori_loop(0, blocks // WIDE_SPAN, step, 0)

    pltpu.emit_pipeline(
        work, grid=(tiles_ref.shape[0] // blocks,),
        in_specs=chunk_specs(blocks, lambda i: i, ((3,), ())),
        out_specs=chunk_specs(blocks, lambda i: i, ((15,),)),
    )(off_ref, cell_ref, out_ref)


def grid_kernel(ends_ref, tiles_ref, lists_ref, counts_ref, up_ref, mid_ref, down_ref,
                before_ref, after_ref, off_hbm, mass_hbm, cell_hbm,
                settled_ref, *refs, row, margin, deals):
    *refs, off_ref, mass_ref, cell_ref, sems = refs
    *piece_refs, rec_down_ref, rec_up_ref, speed_ref = refs
    fetches = [pltpu.make_async_copy(a, b, sems.at[i]) for i, (a, b) in enumerate(
        ((off_hbm, off_ref), (mass_hbm, mass_ref), (cell_hbm, cell_ref)))]
    for fetch in fetches:
        fetch.start()
    rec_refs = (rec_down_ref, rec_up_ref)
    total = settled_ref.shape[0]
    side = before_ref.shape[0]
    inner = side - row
    rid = lax.broadcasted_iota(jnp.int32, (1, 8, LANES), 1)
    pull = jnp.zeros((1, 8, LANES), jnp.float32)
    for k in range(3):
        pull = jnp.where(rid % 4 == k, time_step * gravity_pull[k], pull)

    def speed_of(x):
        mass = jnp.where(rid < 4, x[:, 3:4, :], x[:, 7:8, :])
        return x / jnp.maximum(mass, 1.0) + pull

    chunk = 16
    keep_first = 1.0 - ends_ref[0].astype(jnp.float32)
    keep_last = 1.0 - ends_ref[1].astype(jnp.float32)
    far = row + total - side

    def middle(i, carry):
        at = i * chunk
        speed_ref[pl.ds(row + side + at, chunk)] = speed_of(mid_ref[pl.ds(at, chunk)])
        return carry

    lax.fori_loop(0, mid_ref.shape[0] // chunk, middle, 0)

    def outer(i, carry):
        at = i * chunk
        speed_ref[pl.ds(at, chunk)] = speed_of(before_ref[pl.ds(at, chunk)]) * keep_first
        speed_ref[pl.ds(side + at, chunk)] = speed_of(up_ref[pl.ds(inner + at, chunk)])
        speed_ref[pl.ds(far + at, chunk)] = speed_of(down_ref[pl.ds(at, chunk)])
        speed_ref[pl.ds(row + total + at, chunk)] = (
            speed_of(after_ref[pl.ds(inner + at, chunk)]) * keep_last)
        return carry

    lax.fori_loop(0, row // chunk, outer, 0)

    def seam(i, carry):
        at = i * chunk
        x = speed_of(up_ref[pl.ds(at, chunk)] + before_ref[pl.ds(row + at, chunk)])
        speed_ref[pl.ds(row + at, chunk)] = x * jnp.where(at < margin * row, keep_first, 1.0)
        y = speed_of(down_ref[pl.ds(row + at, chunk)] + after_ref[pl.ds(at, chunk)])
        past = at >= inner - margin * row
        speed_ref[pl.ds(far + row + at, chunk)] = y * jnp.where(past, keep_last, 1.0)
        return carry

    lax.fori_loop(0, inner // chunk, seam, 0)

    def smooth(i, carry):
        at = i * chunk
        s = speed_ref[pl.ds(row + at, chunk)]
        settled_ref[pl.ds(at, chunk)] = s + viscosity * (
            speed_ref[pl.ds(2 * row + at, chunk)] + speed_ref[pl.ds(at, chunk)] - 2.0 * s)
        return carry

    lax.fori_loop(0, total // chunk, smooth, 0)

    flat = settled_ref.reshape(total * 8, LANES)
    planes = piece_refs[0].shape[1]
    across = row // deals
    for turn in range(deals):
        piece_ref = piece_refs[turn]
        corner = lax.rem(ends_ref[2] + turn, deals) * across

        def column(tc, carry, piece_ref=piece_ref, corner=corner):
            for group in range(planes // 8):
                for h in range(2):
                    for k in range(3):
                        start = (margin + group * 8) * row * 8 + (corner + tc) * 8 + h * 4 + k
                        x = flat[pl.ds(start, 8, stride=row * 8), :]
                        at = pl.multiple_of(tc * TILE + h * LANES, LANES)
                        piece_ref[k, group * 8:group * 8 + 8, pl.ds(at, LANES)] = x
            return carry

        lax.fori_loop(0, across, column, 0)

    for fetch in fetches:
        fetch.wait()
    slots = lists_ref.shape[1]

    together = math.gcd(slots, 8)

    def record(n, carry):
        found = []
        for u in range(together):
            i = n * together + u
            for way in range(2):
                b = lists_ref[way, i]
                keep = jnp.where(i < counts_ref[way], 1.0, 0.0)
                c = cell_ref[pl.ds(b, 1), :]
                tile = settled_ref[tiles_ref[b] - ends_ref[3]]
                lane = jnp.broadcast_to(c & (LANES - 1), (8, LANES))
                g = jnp.take_along_axis(tile, lane, axis=1)
                v = jnp.where(c >= LANES, g[4:7], g[0:3])
                o = [off_ref[k, pl.ds(b, 1), :] for k in range(3)]
                found.append((way, i, keep, v, o, mass_ref[pl.ds(b, 1), :]))
        for way, i, keep, v, o, mass in found:
            rec_ref = rec_refs[way]
            for k in range(3):
                rec_ref[i, k:k + 1, :] = (o[k] + time_step * v[k:k + 1]) * keep
                rec_ref[i, pl.ds(6 + k, 3, stride=3), :] = ((-4.0 * v) * o[k]) * keep
            rec_ref[i, 3:6, :] = v * keep
            rec_ref[i, 15:16, :] = mass * keep
        return carry

    lax.fori_loop(0, slots // together, record, 0)


def assemble_kernel(facts_ref, *refs, deals):
    *piece_refs, left_ref, right_ref, grid_ref, arrivals_ref, sems = refs
    planes = piece_refs[0].shape[1]
    copies = []
    for turn, piece_ref in enumerate(piece_refs):
        slot = lax.rem(facts_ref[2] - turn + deals, deals)
        rows = pl.ds(pl.multiple_of(slot * planes, 8), planes)
        for k in range(3):
            copies.append((piece_ref.at[k], grid_ref.at[k, rows, :]))
    copies.append((left_ref, arrivals_ref.at[0]))
    copies.append((right_ref, arrivals_ref.at[1]))
    started = [pltpu.make_async_copy(a, b, sems.at[i]) for i, (a, b) in enumerate(copies)]
    for c in started:
        c.start()
    for c in started:
        c.wait()


def body(offsets, velocity, affine, particle_mass, cell_in_tile, block_tile, live_blocks,
         send_lists, send_counts):
    axes = ("slab", "deal")
    slabs, deals = lax.axis_size("slab"), lax.axis_size("deal")
    count = slabs * deals
    slab, deal = lax.axis_index("slab"), lax.axis_index("deal")
    nb = offsets.shape[0]
    row = PLANE // TILE
    planes = PX // deals
    share = planes * row
    margin = -(-max(share // 16, 1) // row)
    total = (planes + 2 * margin) * row
    side = (2 * margin + 1) * row
    f32 = jnp.float32

    place = slab * deals + deal
    facts = jnp.stack([(place == 0).astype(jnp.int32), (place == count - 1).astype(jnp.int32),
                       deal, deal * share - margin * row, live_blocks[0, 0]])
    mig = send_lists.shape[-1]
    tiles = block_tile
    offsets, velocity, affine = (jnp.transpose(x, (1, 0, 2)) for x in (offsets, velocity, affine))
    blocks = 128 if nb % 128 == 0 else nb
    params = pltpu.CompilerParams(vmem_limit_bytes=VMEM_LIMIT)
    smem = pl.BlockSpec(memory_space=pltpu.SMEM)
    vmem = pl.BlockSpec(memory_space=pltpu.VMEM)
    hbm = pl.BlockSpec(memory_space=pltpu.HBM)
    counter = pltpu.SMEM((1,), jnp.int32)

    def deposit(edges, sizes, name):
        return pl.pallas_call(
            functools.partial(deposit_kernel, blocks=blocks, side=side, total=total, edges=edges),
            in_specs=[smem, smem] + [hbm] * 5,
            out_specs=[vmem] * len(sizes),
            out_shape=[jax.ShapeDtypeStruct((n, 8, LANES), f32) for n in sizes],
            scratch_shapes=[pltpu.VMEM((SPAN * 16, LANES), f32), counter],
            compiler_params=pltpu.CompilerParams(vmem_limit_bytes=DEPOSIT_LIMIT),
            cost_estimate=pl.CostEstimate(flops=nb * 16 * LANES * LANES, transcendentals=0,
                                          bytes_accessed=nb * 17 * LANES * 4),
            name=name,
        )(facts, tiles, offsets, velocity, affine, particle_mass, cell_in_tile)

    up, down = deposit(True, (side, side), "deposit_edges")
    before = lax.ppermute(down, axes, [(i, i + 1) for i in range(count - 1)])
    after = lax.ppermute(up, axes, [(i + 1, i) for i in range(count - 1)])
    mid, = deposit(False, (total - 2 * side,), "deposit_middle")

    width = PLANE // deals
    outs = ([jax.ShapeDtypeStruct((total, 8, LANES), f32)]
            + [jax.ShapeDtypeStruct((3, planes, width), f32)] * deals
            + [jax.ShapeDtypeStruct((mig, 16, LANES), f32)] * 2)
    settled, *pieces, leave_down, leave_up = pl.pallas_call(
        functools.partial(grid_kernel, row=row, margin=margin, deals=deals),
        in_specs=[smem] * 4 + [vmem] * 5 + [hbm] * 3,
        out_specs=[vmem] * len(outs),
        out_shape=outs,
        scratch_shapes=[pltpu.VMEM((total + 2 * row, 8, LANES), f32),
                        pltpu.VMEM((3, nb, LANES), f32), pltpu.VMEM((nb, LANES), f32),
                        pltpu.VMEM((nb, LANES), jnp.int32), pltpu.SemaphoreType.DMA((3,))],
        compiler_params=params,
        name="grid_step",
    )(facts, tiles, send_lists[0, 0], send_counts.reshape(2), up, mid, down, before, after,
      offsets, particle_mass, cell_in_tile)

    for k in range(1, deals):
        pairs = [(i, (i + k) % deals) for i in range(deals)]
        pieces[k] = lax.ppermute(pieces[k], "deal", pairs)
    from_left = lax.ppermute(leave_down, "slab", [(i, i + 1) for i in range(slabs - 1)])
    from_right = lax.ppermute(leave_up, "slab", [(i + 1, i) for i in range(slabs - 1)])

    state = pl.pallas_call(
        functools.partial(update_kernel, blocks=blocks),
        in_specs=[smem, smem, hbm, hbm, vmem],
        out_specs=hbm,
        out_shape=jax.ShapeDtypeStruct((15, nb, LANES), f32),
        scratch_shapes=[pltpu.VMEM((WIDE_SPAN * 8, LANES), f32), counter],
        compiler_params=params,
        cost_estimate=pl.CostEstimate(flops=nb * 15 * LANES * 4,
                                      bytes_accessed=nb * 20 * LANES * 4, transcendentals=0),
        name="update",
    )(facts, tiles, offsets, cell_in_tile, settled)
    state = jnp.transpose(state, (1, 0, 2))

    anywhere = pl.BlockSpec(memory_space=pl.ANY)
    grid, arrivals = pl.pallas_call(
        functools.partial(assemble_kernel, deals=deals),
        in_specs=[smem] + [anywhere] * (deals + 2),
        out_specs=[anywhere] * 2,
        out_shape=[jax.ShapeDtypeStruct((3, PX, width), f32),
                   jax.ShapeDtypeStruct((2, mig, 16, LANES), f32)],
        scratch_shapes=[pltpu.SemaphoreType.DMA((3 * deals + 2,))],
        compiler_params=pltpu.CompilerParams(vmem_limit_bytes=VMEM_LIMIT),
        name="assemble",
    )(facts, *pieces, from_left, from_right)
    arrivals = arrivals[None, None]
    return state, arrivals, grid


def solution(mesh):
    placed = (
        P(("slab", "deal"), None, None),
        P(("slab", "deal"), None, None),
        P(("slab", "deal"), None, None),
        P(("slab", "deal"), None),
        P(("slab", "deal"), None),
        P(("slab", "deal")),
        P("slab", "deal"),
        P("slab", "deal", None, None),
        P("slab", "deal", None),
    )
    return jax.shard_map(
        body,
        mesh=mesh,
        in_specs=placed,
        out_specs=(
            P(("slab", "deal"), None, None),
            P("slab", "deal", None, None, None, None),
            P(None, "slab", "deal"),
        ),
        check_vma=False,
    )
```
